128 devices in a mesh: dp: 16 (over x, z_hi, core), sub: 8 (over z_lo, y).
Axes of the slice: x: 4, y: 4, z: 4 (z_hi: 2, z_lo: 2; z = z_hi * 2 + z_lo), core: 2. Of those that a mesh axis runs over, the one named last changes fastest.
Arguments:
- embeddings: bfloat16 [131072, 1024], P(('dp', 'sub')), may hold values from -4 to 4
- partner: int32 [131072], P(('dp', 'sub')), may hold values from 0 to 131071, as said below
- prior_lse: float32 [131072], P(('dp', 'sub')), may hold values from 4 to 11
Outputs:
- gradient: float32 [131072, 1024], P(('dp', 'sub'))
- row_lse: float32 [131072], P(('dp', 'sub'))
The draws below stay inside these ranges and needn't reach their ends.
Inputs may be any that keep to these rules, and one draw needn't show every extreme that they name: partner[i] lies in the same aligned block of 1024 rows as i and differs from i.
All inputs are finite; a program needn't handle non-finite values.
Results may differ from the reference program's by a relative error of at most 0.0015.
Values may be sent and summed in bfloat16 or wider, within the bound.
A program may use at most 64 MiB of HBM per device.

```python
import math
from functools import reduce
import jax
import jax.numpy as jnp
from jax import lax

D = 1024
ROWS_DEV = 1024
FIRST_STEP = 1
TOTAL = 131072
N_DP = 16
N_SUB = 8


def draw_embeddings(key, part):
    key = jax.random.fold_in(key, 11)
    key_base, key_rows, key_cols = jax.random.split(key, 3)
    row_scale = jnp.exp(jax.random.uniform(key_rows, (TOTAL, 1), jnp.float32, math.log(0.5), math.log(2.0)))
    col_scale = jnp.exp(jax.random.uniform(key_cols, (1, D), jnp.float32, math.log(0.6), math.log(1.6)))
    base = jnp.clip(jax.random.normal(key_base, (TOTAL, D), jnp.float32), -6.0, 6.0) / math.sqrt(D)
    value = base * row_scale * col_scale
    return value.astype(jnp.bfloat16)


def draw_partner(key, part):
    key = jax.random.fold_in(key, 13)
    places = jnp.arange(TOTAL, dtype=jnp.int32)
    offset = jax.random.randint(key, (TOTAL,), 1, ROWS_DEV, dtype=jnp.int32)
    return places // ROWS_DEV * ROWS_DEV + (places % ROWS_DEV + offset) % ROWS_DEV


def draw_prior_lse(key, part):
    key = jax.random.fold_in(key, 17)
    value = 5.0 + 5.0 * jax.random.uniform(key, (TOTAL,), jnp.float32)
    return value.astype(jnp.float32)


def setup_inputs(seed: int = 0) -> dict:
    arg_keys = jax.random.split(jax.random.key(seed), 4)
    embeddings = draw_embeddings(jax.random.fold_in(arg_keys[3], 71), 0)
    partner = draw_partner(jax.random.fold_in(arg_keys[3], 71), 0)
    prior_lse = draw_prior_lse(jax.random.fold_in(arg_keys[3], 71), 0)
    return {"embeddings": embeddings, "partner": partner, "prior_lse": prior_lse}


SCALE = 20.0


def similarity(left, right):
    return SCALE * lax.dot_general(left, right, (((1,), (1,)), ((), ())), preferred_element_type=jnp.float32)


def masked_self(block):
    scores = similarity(block, block)
    count = scores.shape[0]
    diagonal = lax.broadcasted_iota(jnp.int32, (count, count), 0) == lax.broadcasted_iota(jnp.int32, (count, count), 1)
    return jnp.where(diagonal, -jnp.inf, scores)


def row_extrema(scores):
    peak = jnp.max(scores, axis=1)
    total = jnp.sum(jnp.exp(scores - peak[:, None]), axis=1)
    return peak, total


def merge_stats(pairs):
    peak = reduce(jnp.maximum, [entry[0] for entry in pairs])
    total = reduce(jnp.add, [entry[1] * jnp.exp(entry[0] - peak) for entry in pairs])
    return peak + jnp.log(total)


def self_weights(own_tile, lse_rows, local_pos):
    count = own_tile.shape[0]
    onehot = (local_pos[:, None] == lax.broadcasted_iota(jnp.int32, (count, count), 1)).astype(jnp.float32)
    chances = jnp.exp(own_tile - lse_rows[:, None]) - onehot
    return (chances + chances.T).astype(jnp.bfloat16)


def pair_weights(scores, lse_rows, other_lse):
    return (jnp.exp(scores - lse_rows[:, None]) + jnp.exp(scores - other_lse[None, :])).astype(jnp.bfloat16)


def reference(embeddings, partner, prior_lse):
    count = N_DP * N_SUB
    distances = (FIRST_STEP, N_SUB + 1)
    blocks = embeddings.reshape(count, ROWS_DEV, D)
    prior_blocks = prior_lse.reshape(count, ROWS_DEV)
    partner_blocks = partner.reshape(count, ROWS_DEV)
    positions = jnp.arange(count, dtype=jnp.int32)

    def forward(index):
        own_block = blocks[index]
        pairs = [row_extrema(masked_self(own_block)), (prior_blocks[index], jnp.ones((ROWS_DEV,), jnp.float32))]
        for step in distances:
            for sign in (1, -1):
                other = blocks[((index + sign * step) % count).astype(jnp.int32)]
                pairs.append(row_extrema(similarity(own_block, other)))
        return merge_stats(pairs)

    lse_blocks = lax.map(forward, positions)

    def backward(index):
        own_block = blocks[index]
        own_lse = lse_blocks[index]
        local_pos = (partner_blocks[index] % ROWS_DEV).astype(jnp.int32)
        total = jnp.dot(self_weights(masked_self(own_block), own_lse, local_pos), own_block, preferred_element_type=jnp.float32)
        for step in distances:
            place = ((index + step) % count).astype(jnp.int32)
            other = blocks[place]
            weights = pair_weights(similarity(own_block, other), own_lse, lse_blocks[place])
            total = total + jnp.dot(weights, other, preferred_element_type=jnp.float32)
        for step in distances:
            place = ((index - step) % count).astype(jnp.int32)
            other = blocks[place]
            weights = pair_weights(similarity(own_block, other), own_lse, lse_blocks[place])
            term = jnp.dot(weights, other, preferred_element_type=jnp.float32)
            total = total + lax.optimization_barrier(term.astype(jnp.bfloat16)).astype(jnp.float32)
        return SCALE * total

    gradient = lax.map(backward, positions).reshape(TOTAL, D)
    return gradient, lse_blocks.reshape(TOTAL)
```

```python
import functools
import math

import jax
import jax.numpy as jnp
from jax import lax
from jax.experimental import pallas as pl
from jax.experimental.pallas import tpu as pltpu
from jax.sharding import PartitionSpec as P

MESH = pl.DeviceIdType.MESH
BLOCKS = 128
ROWS = 1024
D = 1024
SCALE = 20.0
LOG2E = math.log2(math.e)
LN2 = math.log(2.0)
CHUNKS = 16
R = ROWS // CHUNKS
GROUP = 256
PER_GROUP = GROUP // R
LAG = 5
BEHIND = 8
MASKED = -1e37
M1, P1, M9, P9, RL, RZ = range(6)


def coords(b):
    dp, sub = b // 8, b % 8
    return dp // 4, sub % 4, (dp // 2) % 2 * 2 + sub // 4, dp % 2


def block_at(x, y, z, c):
    return ((x * 2 + z // 2) * 2 + c) * 8 + (z % 2) * 4 + y


def device(b):
    return (b // 8, b % 8)


def core(b):
    return (b // 8) % 2


def near(b, step):
    return (b + BLOCKS + step) % BLOCKS


def in_column(b, y):
    x, _, z, c = coords(b)
    return block_at(x, y, z, c)


def kernel(
    e_hbm, partner_ref, prior_ref, grad_hbm, lse_ref,
    own, buf, scores, out, peak, total, lcol, pcol, lnb,
    load_sem, store_sem, s_up, s_dn, s_far, s_r9, s_r1, s_z, s_loc, s_lse, r_lse, recv,
):
    b = lax.axis_index("dp") * 8 + lax.axis_index("sub")
    x, y, z, c = coords(b)
    up, dn = block_at(x, (y + 1) % 4, z, c), block_at(x, (y + 3) % 4, z, c)
    mate = block_at(x, y, z, 1 - c)
    y0, y3 = y == 0, y == 3

    load = pltpu.make_async_copy(e_hbm, own, load_sem)
    load.start()

    barrier = pltpu.get_barrier_semaphore()

    def greet(t):
        pl.semaphore_signal(barrier, inc=1, device_id=device(t), device_id_type=MESH)

    for t in (up, dn, near(b, 1), near(b, -1), near(b, 9), near(b, -9), near(b, 8), near(b, -8)):
        greet(t)

    @pl.when(y0)
    def _():
        greet(in_column(near(b, -1), 0))
        greet(in_column(near(b, -9), 0))
        greet(in_column(near(b, -1), 0))
        greet(near(in_column(b, 3), 1))

    @pl.when(y3)
    def _():
        greet(in_column(near(b, 1), 3))
        greet(in_column(near(b, 9), 3))
        greet(in_column(near(b, 1), 3))
        greet(near(in_column(b, 0), -1))

    pl.semaphore_wait(barrier, 8 + jnp.where(y0 | y3, 4, 0))

    up_dbl, up_sgl = y3 & (core(near(b, 1)) == 1), y3 & (core(near(b, 1)) == 0)
    dn_dbl, dn_sgl = y0 & (core(near(b, -1)) == 0), y0 & (core(near(b, -1)) == 1)
    q1 = jnp.where(y0, near(dn, 1), near(up, -1))
    q9 = jnp.where(y0, near(dn, 9), near(up, -9))
    wrap = y0 | y3
    rel_dbl = (y0 & (core(q1) == 1)) | (y3 & (core(q1) == 0))
    rel_sgl = wrap & ~rel_dbl
    rel_z = (y3 & (c == 0)) | (y0 & (c == 1))
    do_far = ((~y0) & (c == 1)) | ((~y3) & (c == 0))
    loc_late = (y0 & (c == 0)) | (y3 & (c == 1))
    near_slot, far_slot = jnp.where(y0, M1, P1), jnp.where(y0, M9, P9)

    def rows(k):
        return pl.ds(pl.multiple_of(k * R, R), R)

    def copy(src, to, slot, k, sem):
        return pltpu.make_async_remote_copy(
            src_ref=src, dst_ref=buf.at[slot, rows(k)], send_sem=sem, recv_sem=recv.at[slot, k],
            device_id=device(to), device_id_type=MESH,
        )

    def held(slot, k):
        return buf.at[slot, rows(k)]

    def arrived(slot, k):
        pltpu.make_async_copy(held(slot, k), held(slot, k), recv.at[slot, k]).wait()

    def send_up(k):
        odd = k % 2 == 1
        to = jnp.where(up_sgl & odd, in_column(near(b, 1), 3), up)
        slot = jnp.where(y3, jnp.where(up_sgl & odd, RZ, RL), M1)
        return copy(e_hbm.at[rows(k)], to, slot, k, s_up.at[k])

    def send_dn(k):
        odd = k % 2 == 1
        to = jnp.where(dn_sgl & odd, in_column(near(b, -1), 0), dn)
        slot = jnp.where(y0, jnp.where(dn_sgl & odd, RZ, RL), P1)
        return copy(e_hbm.at[rows(k)], to, slot, k, s_dn.at[k])

    def send_far(k):
        return copy(
            held(jnp.where(c == 1, M1, P1), k), jnp.where(c == 1, near(b, 8), near(b, -8)),
            jnp.where(c == 1, M9, P9), k, s_far.at[k],
        )

    def send_r1(k):
        return copy(held(RL, k), q1, near_slot, k, s_r1.at[k])

    def send_r9(k):
        return copy(held(RL, k), q9, far_slot, k, s_r9.at[k])

    def send_z(k):
        return copy(held(RZ, k), jnp.where(y3, up, dn), jnp.where(y3, M1, P1), k, s_z.at[k])

    def send_loc(k):
        return copy(held(jnp.where(c == 0, M1, P1), k), mate, jnp.where(c == 0, M9, P9), k, s_loc.at[k])

    def start_own(k, carry):
        send_up(k).start()
        send_dn(k).start()
        return carry

    lax.fori_loop(0, CHUNKS, start_own, 0)

    load.wait()

    def column(row):
        return jnp.transpose(jnp.broadcast_to(row, (128, ROWS)))

    pcol[...] = column((partner_ref[...] % ROWS).astype(jnp.float32))

    def scored(left, right):
        return (SCALE * LOG2E) * lax.dot_general(
            left, right, (((1,), (1,)), ((), ())), preferred_element_type=jnp.float32
        )

    def own_scores(g, carry):
        cols = pl.ds(pl.multiple_of(g * GROUP, GROUP), GROUP)
        tile = scored(own[...], own[cols, :])
        diagonal = lax.broadcasted_iota(jnp.int32, tile.shape, 0) == (
            lax.broadcasted_iota(jnp.int32, tile.shape, 1) + g * GROUP
        )
        scores[4, :, cols] = jnp.where(diagonal, MASKED, tile)
        return carry

    lax.fori_loop(0, ROWS // GROUP, own_scores, 0)

    def own_stats(r, carry):
        at = pl.ds(pl.multiple_of(r * 64, 64), 64)
        top = scores[4, at, 0:128]
        for i in range(1, 8):
            top = jnp.maximum(top, scores[4, at, i * 128 : (i + 1) * 128])
        acc = jnp.exp2(scores[4, at, 0:128] - top)
        for i in range(1, 8):
            acc = acc + jnp.exp2(scores[4, at, i * 128 : (i + 1) * 128] - top)
        peak[at, :] = top
        total[at, :] = acc
        return carry

    lax.fori_loop(0, ROWS // 64, own_stats, 0)

    def step(k, carry):
        @pl.when(k < CHUNKS)
        def _():
            odd = k % 2 == 1

            @pl.when(rel_dbl)
            def _():
                arrived(RL, k)
                send_r1(k).start()
                send_r9(k).start()

            @pl.when(rel_sgl & ~odd)
            def _():
                arrived(RL, k)
                send_r1(k).start()

            @pl.when(rel_z & odd)
            def _():
                arrived(RZ, k)
                send_z(k).start()

            @pl.when(~y0)
            def _():
                arrived(M1, k)

            @pl.when(~y3)
            def _():
                arrived(P1, k)

            @pl.when(do_far)
            def _():
                send_far(k).start()

            @pl.when(~loc_late)
            def _():
                send_loc(k).start()

        @pl.when((k >= LAG) & (k < CHUNKS + LAG))
        def _():
            j = k - LAG

            @pl.when(y0)
            def _():
                arrived(M1, j)

            @pl.when(y3)
            def _():
                arrived(P1, j)

            @pl.when(loc_late)
            def _():
                send_loc(j).start()

        @pl.when(k >= BEHIND)
        def _():
            item = k - BEHIND
            g, t = item // 4, item % 4

            @pl.when(t >= 2)
            def _():
                for i in range(PER_GROUP):
                    arrived(t, g * PER_GROUP + i)

            cols = pl.ds(pl.multiple_of(g * GROUP, GROUP), GROUP)
            scores[t, :, cols] = scored(own[...], buf[t, cols, :])

            def stats(r, carry):
                at = pl.ds(pl.multiple_of(r * 128, 128), 128)
                tile = scores[t, at, cols]
                old = peak[at, :]
                top = jnp.maximum(old, jnp.maximum(tile[:, :128], tile[:, 128:]))
                peak[at, :] = top
                total[at, :] = (
                    total[at, :] * jnp.exp2(old - top) + jnp.exp2(tile[:, :128] - top) + jnp.exp2(tile[:, 128:] - top)
                )
                return carry

            lax.fori_loop(0, ROWS // 128, stats, 0, unroll=2)

        return carry

    lax.fori_loop(0, CHUNKS + BEHIND, step, 0)

    prior = column(prior_ref[...] * LOG2E)
    lane_peak = peak[...]
    top = jnp.broadcast_to(jnp.max(lane_peak, axis=1, keepdims=True), (ROWS, 128))
    summed = jnp.sum(total[...] * jnp.exp2(lane_peak - top), axis=1, keepdims=True)
    both = jnp.maximum(top, prior)
    lse2 = both + jnp.log2(summed * jnp.exp2(top - both) + jnp.exp2(prior - both))
    lcol[...] = lse2
    lnb[4] = jnp.transpose(lse2)[0:8, :]
    lse_ref[...] = lnb[4, 0:1, :] * LN2

    def send_lse(t, to):
        return pltpu.make_async_remote_copy(
            src_ref=lnb.at[4], dst_ref=lnb.at[t], send_sem=s_lse.at[t], recv_sem=r_lse.at[t],
            device_id=device(to), device_id_type=MESH,
        )

    lse_sends = [send_lse(M1, near(b, 1)), send_lse(P1, near(b, -1)), send_lse(M9, near(b, 9)), send_lse(P9, near(b, -9))]
    for s in lse_sends:
        s.start()

    def weights(t, at):
        parts = []
        mine = lcol[at, :]
        for i in range(8):
            lanes = slice(i * 128, (i + 1) * 128)
            tile = scores[t, at, lanes]
            parts.append(jnp.exp2(tile - mine) + jnp.exp2(tile - lnb[t, 0:1, lanes]))
        return parts

    prow = (partner_ref[...] % ROWS).astype(jnp.float32)

    def own_part(r, carry):
        at = pl.ds(pl.multiple_of(r * 256, 256), 256)
        parts = weights(4, at)
        mine = pcol[at, :]
        row = (lax.broadcasted_iota(jnp.int32, (256, 128), 0) + r * 256).astype(jnp.float32)
        lane = lax.broadcasted_iota(jnp.int32, (256, 128), 1).astype(jnp.float32)
        for i in range(8):
            lanes = slice(i * 128, (i + 1) * 128)
            hot = jnp.where(mine == lane + i * 128.0, 1.0, 0.0) + jnp.where(prow[:, lanes] == row, 1.0, 0.0)
            parts[i] = (parts[i] - hot).astype(jnp.bfloat16)
        out[at, :] = jnp.dot(jnp.concatenate(parts, axis=1), own[...], preferred_element_type=jnp.float32)
        return carry

    lax.fori_loop(0, 4, own_part, 0)

    for s in lse_sends:
        s.wait_recv()

    def rest(r, carry):
        at = pl.ds(pl.multiple_of(r * 256, 256), 256)
        acc = out[at, :]
        for t in (P1, P9, M1, M9):
            w = jnp.concatenate([p.astype(jnp.bfloat16) for p in weights(t, at)], axis=1)
            term = jnp.dot(w, buf[t], preferred_element_type=jnp.float32)
            if t in (M1, M9):
                term = term.astype(jnp.bfloat16).astype(jnp.float32)
            acc = acc + term
        out[at, :] = SCALE * acc
        pltpu.make_async_copy(out.at[at], grad_hbm.at[at], store_sem.at[r]).start()
        return carry

    lax.fori_loop(0, 4, rest, 0)

    for s in lse_sends:
        s.wait_send()

    def sent(k, carry):
        odd = k % 2 == 1
        send_up(k).wait_send()
        send_dn(k).wait_send()
        send_loc(k).wait_send()

        @pl.when(do_far)
        def _():
            send_far(k).wait_send()

        @pl.when(rel_dbl)
        def _():
            send_r1(k).wait_send()
            send_r9(k).wait_send()

        @pl.when(rel_sgl & ~odd)
        def _():
            send_r1(k).wait_send()

        @pl.when(rel_z & odd)
        def _():
            send_z(k).wait_send()

        return carry

    lax.fori_loop(0, CHUNKS, sent, 0)

    def stored(r, carry):
        at = pl.ds(pl.multiple_of(r * 256, 256), 256)
        pltpu.make_async_copy(out.at[at], grad_hbm.at[at], store_sem.at[r]).wait()
        return carry

    lax.fori_loop(0, 4, stored, 0)


def per_device(embeddings, partner, prior_lse):
    dma = pltpu.SemaphoreType.DMA
    f32 = jnp.float32
    gradient, lse = pl.pallas_call(
        kernel,
        out_shape=(jax.ShapeDtypeStruct((ROWS, D), f32), jax.ShapeDtypeStruct((1, ROWS), f32)),
        in_specs=[
            pl.BlockSpec(memory_space=pl.ANY),
            pl.BlockSpec(memory_space=pltpu.VMEM),
            pl.BlockSpec(memory_space=pltpu.VMEM),
        ],
        out_specs=(pl.BlockSpec(memory_space=pl.ANY), pl.BlockSpec(memory_space=pltpu.VMEM)),
        scratch_shapes=[
            pltpu.VMEM((ROWS, D), jnp.bfloat16),
            pltpu.VMEM((6, ROWS, D), jnp.bfloat16),
            pltpu.VMEM((5, ROWS, ROWS), f32),
            pltpu.VMEM((ROWS, D), f32),
            pltpu.VMEM((ROWS, 128), f32),
            pltpu.VMEM((ROWS, 128), f32),
            pltpu.VMEM((ROWS, 128), f32),
            pltpu.VMEM((ROWS, 128), f32),
            pltpu.VMEM((5, 8, ROWS), f32),
            dma, dma((4,)), dma((CHUNKS,)), dma((CHUNKS,)), dma((CHUNKS,)), dma((CHUNKS,)), dma((CHUNKS,)),
            dma((CHUNKS,)), dma((CHUNKS,)), dma((4,)), dma((4,)), dma((6, CHUNKS)),
        ],
        compiler_params=pltpu.CompilerParams(collective_id=0, has_side_effects=True, vmem_limit_bytes=56 << 20),
        cost_estimate=pl.CostEstimate(flops=20 * ROWS * ROWS * D, bytes_accessed=8 << 20, transcendentals=20 << 20),
    )(embeddings, partner.reshape(1, ROWS), prior_lse.reshape(1, ROWS))
    return gradient, lse.reshape(ROWS)


def solution(mesh):
    placed = (P(("dp", "sub"), None), P(("dp", "sub")), P(("dp", "sub")))
    return jax.shard_map(
        per_device,
        mesh=mesh,
        in_specs=placed,
        out_specs=(P(("dp", "sub"), None), P(("dp", "sub"))),
        check_vma=False,
    )
```

```python
import functools
import math

import jax
import jax.numpy as jnp
from jax import lax
from jax.experimental import pallas as pl
from jax.experimental.pallas import tpu as pltpu
from jax.sharding import PartitionSpec as P

MESH = pl.DeviceIdType.MESH
BLOCKS = 128
ROWS = 1024
D = 1024
SCALE = 20.0
LOG2E = math.log2(math.e)
LN2 = math.log(2.0)
CHUNKS = 16
R = ROWS // CHUNKS
GROUP = 256
PER_GROUP = GROUP // R
LAG = 5
BEHIND = 8
MASKED = -1e37
M1, P1, M9, P9, RL, RZ = range(6)


def coords(b):
    dp, sub = b // 8, b % 8
    return dp // 4, sub % 4, (dp // 2) % 2 * 2 + sub // 4, dp % 2


def block_at(x, y, z, c):
    return ((x * 2 + z // 2) * 2 + c) * 8 + (z % 2) * 4 + y


def device(b):
    return (b // 8, b % 8)


def core(b):
    return (b // 8) % 2


def near(b, step):
    return (b + BLOCKS + step) % BLOCKS


def in_column(b, y):
    x, _, z, c = coords(b)
    return block_at(x, y, z, c)


def kernel(
    e_hbm, partner_ref, prior_ref, grad_hbm, lse_ref,
    own, buf, scores, out, peak, total, lcol, pcol, lnb,
    load_sem, store_sem, s_up, s_dn, s_far, s_r9, s_r1, s_z, s_loc, s_lse, r_lse, recv,
):
    b = lax.axis_index("dp") * 8 + lax.axis_index("sub")
    x, y, z, c = coords(b)
    up, dn = block_at(x, (y + 1) % 4, z, c), block_at(x, (y + 3) % 4, z, c)
    mate = block_at(x, y, z, 1 - c)
    y0, y3 = y == 0, y == 3

    load = pltpu.make_async_copy(e_hbm, own, load_sem)
    load.start()

    barrier = pltpu.get_barrier_semaphore()

    def greet(t):
        pl.semaphore_signal(barrier, inc=1, device_id=device(t), device_id_type=MESH)

    for t in (up, dn, mate, near(b, 16 * c - 8)):
        greet(t)

    @pl.when(y0)
    def _():
        greet(in_column(near(b, -1), 0))
        greet(in_column(near(b, -9), 0))
        greet(in_column(near(b, -1), 0))
        greet(near(in_column(b, 3), 1))

    @pl.when(y3)
    def _():
        greet(in_column(near(b, 1), 3))
        greet(in_column(near(b, 9), 3))
        greet(in_column(near(b, 1), 3))
        greet(near(in_column(b, 0), -1))

    z_src = ((y == 1) & (c == 0)) | ((y == 2) & (c == 1))
    z_mid = ((y == 1) & (c == 1)) | ((y == 2) & (c == 0))

    @pl.when(z_mid)
    def _():
        greet(jnp.where(y == 1, near(in_column(b, 0), 9), near(in_column(b, 3), -9)))

    pl.semaphore_wait(barrier, 4 + jnp.where(y0 | y3, 4, 0) + jnp.where(z_src, 1, 0))

    up_dbl, up_sgl = y3 & (core(near(b, 1)) == 1), y3 & (core(near(b, 1)) == 0)
    dn_dbl, dn_sgl = y0 & (core(near(b, -1)) == 0), y0 & (core(near(b, -1)) == 1)
    q1 = jnp.where(y0, near(dn, 1), near(up, -1))
    q9 = jnp.where(y0, near(dn, 9), near(up, -9))
    wrap = y0 | y3
    rel_dbl = (y0 & (core(q1) == 1)) | (y3 & (core(q1) == 0))
    rel_sgl = wrap & ~rel_dbl
    rel_z = (y3 & (c == 0)) | (y0 & (c == 1))
    do_far = ((~y0) & (c == 1)) | ((~y3) & (c == 0))
    loc_late = (y0 & (c == 0)) | (y3 & (c == 1))
    near_slot, far_slot = jnp.where(y0, M1, P1), jnp.where(y0, M9, P9)

    def rows(k):
        return pl.ds(pl.multiple_of(k * R, R), R)

    def copy(src, to, slot, k, sem):
        return pltpu.make_async_remote_copy(
            src_ref=src, dst_ref=buf.at[slot, rows(k)], send_sem=sem, recv_sem=recv.at[slot, k],
            device_id=device(to), device_id_type=MESH,
        )

    def held(slot, k):
        return buf.at[slot, rows(k)]

    def arrived(slot, k):
        pltpu.make_async_copy(held(slot, k), held(slot, k), recv.at[slot, k]).wait()

    def send_up(k):
        odd = k % 2 == 1
        to = jnp.where(up_sgl & odd, in_column(near(b, 1), 3), up)
        slot = jnp.where(y3, jnp.where(up_sgl & odd, RZ, RL), M1)
        return copy(e_hbm.at[rows(k)], to, slot, k, s_up.at[k])

    def send_dn(k):
        odd = k % 2 == 1
        to = jnp.where(dn_sgl & odd, in_column(near(b, -1), 0), dn)
        slot = jnp.where(y0, jnp.where(dn_sgl & odd, RZ, RL), P1)
        return copy(e_hbm.at[rows(k)], to, slot, k, s_dn.at[k])

    def send_far(k):
        return copy(
            held(jnp.where(c == 1, M1, P1), k), jnp.where(c == 1, near(b, 8), near(b, -8)),
            jnp.where(c == 1, M9, P9), k, s_far.at[k],
        )

    def send_r1(k):
        return copy(held(RL, k), q1, near_slot, k, s_r1.at[k])

    def send_r9(k):
        return copy(held(RL, k), q9, far_slot, k, s_r9.at[k])

    def send_z(k):
        ahead = (y == 0) | (y == 1)
        slot = jnp.where(y3, M1, jnp.where(y0, P1, jnp.where(y == 1, P9, M9)))
        return copy(held(RZ, k), jnp.where(ahead, dn, up), slot, k, s_z.at[k])

    def send_side(k):
        to = jnp.where(y == 1, in_column(near(b, -9), 1), in_column(near(b, 9), 2))
        return copy(e_hbm.at[rows(k)], to, RZ, k, s_z.at[k])

    def send_loc(k):
        return copy(held(jnp.where(c == 0, M1, P1), k), mate, jnp.where(c == 0, M9, P9), k, s_loc.at[k])

    def z_moves(k):
        return (rel_z & (k % 2 == 1)) | (z_mid & (k % 4 == 3))

    def far_moves(k):
        return do_far & ~(wrap & (k % 4 == 3))

    def start_own(k, carry):
        @pl.when(z_src & (k % 4 == 3))
        def _():
            send_side(k).start()

        send_up(k).start()
        send_dn(k).start()
        return carry

    lax.fori_loop(0, CHUNKS, start_own, 0)

    load.wait()

    def column(row):
        return jnp.transpose(jnp.broadcast_to(row, (128, ROWS)))

    pcol[...] = column((partner_ref[...] % ROWS).astype(jnp.float32))

    def scored(left, right):
        return (SCALE * LOG2E) * lax.dot_general(
            left, right, (((1,), (1,)), ((), ())), preferred_element_type=jnp.float32
        )

    def own_scores(g, carry):
        cols = pl.ds(pl.multiple_of(g * GROUP, GROUP), GROUP)
        tile = scored(own[...], own[cols, :])
        diagonal = lax.broadcasted_iota(jnp.int32, tile.shape, 0) == (
            lax.broadcasted_iota(jnp.int32, tile.shape, 1) + g * GROUP
        )
        scores[4, :, cols] = jnp.where(diagonal, MASKED, tile)
        return carry

    lax.fori_loop(0, ROWS // GROUP, own_scores, 0)

    def own_stats(r, carry):
        at = pl.ds(pl.multiple_of(r * 64, 64), 64)
        top = scores[4, at, 0:128]
        for i in range(1, 8):
            top = jnp.maximum(top, scores[4, at, i * 128 : (i + 1) * 128])
        acc = jnp.exp2(scores[4, at, 0:128] - top)
        for i in range(1, 8):
            acc = acc + jnp.exp2(scores[4, at, i * 128 : (i + 1) * 128] - top)
        peak[at, :] = top
        total[at, :] = acc
        return carry

    lax.fori_loop(0, ROWS // 64, own_stats, 0)

    def step(k, carry):
        @pl.when(k < CHUNKS)
        def _():
            odd = k % 2 == 1

            @pl.when(rel_dbl)
            def _():
                arrived(RL, k)
                send_r1(k).start()
                send_r9(k).start()

            @pl.when(rel_sgl & ~odd)
            def _():
                arrived(RL, k)
                send_r1(k).start()

            @pl.when(z_moves(k))
            def _():
                arrived(RZ, k)
                send_z(k).start()

            @pl.when(~y0)
            def _():
                arrived(M1, k)

            @pl.when(~y3)
            def _():
                arrived(P1, k)

            @pl.when(far_moves(k))
            def _():
                send_far(k).start()

            @pl.when(~loc_late)
            def _():
                send_loc(k).start()

        @pl.when((k >= LAG) & (k < CHUNKS + LAG))
        def _():
            j = k - LAG

            @pl.when(y0)
            def _():
                arrived(M1, j)

            @pl.when(y3)
            def _():
                arrived(P1, j)

            @pl.when(loc_late)
            def _():
                send_loc(j).start()

        @pl.when(k >= BEHIND)
        def _():
            item = k - BEHIND
            g, t = item // 4, item % 4

            @pl.when(t >= 2)
            def _():
                for i in range(PER_GROUP):
                    arrived(t, g * PER_GROUP + i)

            cols = pl.ds(pl.multiple_of(g * GROUP, GROUP), GROUP)
            scores[t, :, cols] = scored(own[...], buf[t, cols, :])

            def stats(r, carry):
                at = pl.ds(pl.multiple_of(r * 128, 128), 128)
                tile = scores[t, at, cols]
                old = peak[at, :]
                top = jnp.maximum(old, jnp.maximum(tile[:, :128], tile[:, 128:]))
                peak[at, :] = top
                total[at, :] = (
                    total[at, :] * jnp.exp2(old - top) + jnp.exp2(tile[:, :128] - top) + jnp.exp2(tile[:, 128:] - top)
                )
                return carry

            lax.fori_loop(0, ROWS // 128, stats, 0, unroll=2)

        return carry

    lax.fori_loop(0, CHUNKS + BEHIND, step, 0)

    prior = column(prior_ref[...] * LOG2E)
    lane_peak = peak[...]
    top = jnp.broadcast_to(jnp.max(lane_peak, axis=1, keepdims=True), (ROWS, 128))
    summed = jnp.sum(total[...] * jnp.exp2(lane_peak - top), axis=1, keepdims=True)
    both = jnp.maximum(top, prior)
    lse2 = both + jnp.log2(summed * jnp.exp2(top - both) + jnp.exp2(prior - both))
    lcol[...] = lse2
    lnb[4] = jnp.transpose(lse2)[0:8, :]
    lse_ref[...] = lnb[4, 0:1, :] * LN2

    def send_lse(t, to):
        return pltpu.make_async_remote_copy(
            src_ref=lnb.at[4], dst_ref=lnb.at[t], send_sem=s_lse.at[t], recv_sem=r_lse.at[t],
            device_id=device(to), device_id_type=MESH,
        )

    lse_sends = [send_lse(M1, near(b, 1)), send_lse(P1, near(b, -1)), send_lse(M9, near(b, 9)), send_lse(P9, near(b, -9))]
    for s in lse_sends:
        s.start()

    def weights(t, at):
        parts = []
        mine = lcol[at, :]
        for i in range(8):
            lanes = slice(i * 128, (i + 1) * 128)
            tile = scores[t, at, lanes]
            parts.append(jnp.exp2(tile - mine) + jnp.exp2(tile - lnb[t, 0:1, lanes]))
        return parts

    prow = (partner_ref[...] % ROWS).astype(jnp.float32)

    def own_part(r, carry):
        at = pl.ds(pl.multiple_of(r * 256, 256), 256)
        parts = weights(4, at)
        mine = pcol[at, :]
        row = (lax.broadcasted_iota(jnp.int32, (256, 128), 0) + r * 256).astype(jnp.float32)
        lane = lax.broadcasted_iota(jnp.int32, (256, 128), 1).astype(jnp.float32)
        for i in range(8):
            lanes = slice(i * 128, (i + 1) * 128)
            hot = jnp.where(mine == lane + i * 128.0, 1.0, 0.0) + jnp.where(prow[:, lanes] == row, 1.0, 0.0)
            parts[i] = (parts[i] - hot).astype(jnp.bfloat16)
        out[at, :] = jnp.dot(jnp.concatenate(parts, axis=1), own[...], preferred_element_type=jnp.float32)
        return carry

    lax.fori_loop(0, 4, own_part, 0)

    for s in lse_sends:
        s.wait_recv()

    def rest(r, carry):
        at = pl.ds(pl.multiple_of(r * 256, 256), 256)
        acc = out[at, :]
        for t in (P1, P9, M1, M9):
            w = jnp.concatenate([p.astype(jnp.bfloat16) for p in weights(t, at)], axis=1)
            term = jnp.dot(w, buf[t], preferred_element_type=jnp.float32)
            if t in (M1, M9):
                term = term.astype(jnp.bfloat16).astype(jnp.float32)
            acc = acc + term
        out[at, :] = SCALE * acc
        pltpu.make_async_copy(out.at[at], grad_hbm.at[at], store_sem.at[r]).start()
        return carry

    lax.fori_loop(0, 4, rest, 0)

    for s in lse_sends:
        s.wait_send()

    def sent(k, carry):
        odd = k % 2 == 1
        send_up(k).wait_send()
        send_dn(k).wait_send()
        send_loc(k).wait_send()

        @pl.when(far_moves(k))
        def _():
            send_far(k).wait_send()

        @pl.when(rel_dbl)
        def _():
            send_r1(k).wait_send()
            send_r9(k).wait_send()

        @pl.when(rel_sgl & ~odd)
        def _():
            send_r1(k).wait_send()

        @pl.when(z_src & (k % 4 == 3))
        def _():
            send_side(k).wait_send()

        @pl.when(z_moves(k))
        def _():
            send_z(k).wait_send()

        return carry

    lax.fori_loop(0, CHUNKS, sent, 0)

    def stored(r, carry):
        at = pl.ds(pl.multiple_of(r * 256, 256), 256)
        pltpu.make_async_copy(out.at[at], grad_hbm.at[at], store_sem.at[r]).wait()
        return carry

    lax.fori_loop(0, 4, stored, 0)


def per_device(embeddings, partner, prior_lse):
    dma = pltpu.SemaphoreType.DMA
    f32 = jnp.float32
    gradient, lse = pl.pallas_call(
        kernel,
        out_shape=(pltpu.VMEM((ROWS, D), f32), jax.ShapeDtypeStruct((1, ROWS), f32)),
        in_specs=[
            pl.BlockSpec(memory_space=pl.ANY),
            pl.BlockSpec(memory_space=pltpu.VMEM),
            pl.BlockSpec(memory_space=pltpu.VMEM),
        ],
        out_specs=(pl.BlockSpec(memory_space=pl.ANY), pl.BlockSpec(memory_space=pltpu.VMEM)),
        scratch_shapes=[
            pltpu.VMEM((ROWS, D), jnp.bfloat16),
            pltpu.VMEM((6, ROWS, D), jnp.bfloat16),
            pltpu.VMEM((5, ROWS, ROWS), f32),
            pltpu.VMEM((ROWS, D), f32),
            pltpu.VMEM((ROWS, 128), f32),
            pltpu.VMEM((ROWS, 128), f32),
            pltpu.VMEM((ROWS, 128), f32),
            pltpu.VMEM((ROWS, 128), f32),
            pltpu.VMEM((5, 8, ROWS), f32),
            dma, dma((4,)), dma((CHUNKS,)), dma((CHUNKS,)), dma((CHUNKS,)), dma((CHUNKS,)), dma((CHUNKS,)),
            dma((CHUNKS,)), dma((CHUNKS,)), dma((4,)), dma((4,)), dma((6, CHUNKS)),
        ],
        compiler_params=pltpu.CompilerParams(collective_id=0, has_side_effects=True, vmem_limit_bytes=56 << 20),
        cost_estimate=pl.CostEstimate(flops=20 * ROWS * ROWS * D, bytes_accessed=8 << 20, transcendentals=20 << 20),
    )(embeddings, partner.reshape(1, ROWS), prior_lse.reshape(1, ROWS))
    return gradient, lse.reshape(ROWS)


def solution(mesh):
    placed = (P(("dp", "sub"), None), P(("dp", "sub")), P(("dp", "sub")))
    return jax.shard_map(
        per_device,
        mesh=mesh,
        in_specs=placed,
        out_specs=(P(("dp", "sub"), None), P(("dp", "sub"))),
        check_vma=False,
    )
```

```python
import functools
import math

import jax
import jax.numpy as jnp
from jax import lax
from jax.experimental import pallas as pl
from jax.experimental.pallas import tpu as pltpu
from jax.sharding import PartitionSpec as P

MESH = pl.DeviceIdType.MESH
BLOCKS = 128
ROWS = 1024
D = 1024
SCALE = 20.0
LOG2E = math.log2(math.e)
LN2 = math.log(2.0)
CHUNKS = 16
AHEAD = 4
PACE = CHUNKS // 16
R = ROWS // CHUNKS
GROUP = 256
PER_GROUP = GROUP // R
LAG = 5 * PACE
BEHIND = 8 * PACE
MASKED = -1e37
M1, P1, M9, P9, RL, RZ = range(6)


def coords(b):
    dp, sub = b // 8, b % 8
    return dp // 4, sub % 4, (dp // 2) % 2 * 2 + sub // 4, dp % 2


def block_at(x, y, z, c):
    return ((x * 2 + z // 2) * 2 + c) * 8 + (z % 2) * 4 + y


def device(b):
    return (b // 8, b % 8)


def core(b):
    return (b // 8) % 2


def near(b, step):
    return (b + BLOCKS + step) % BLOCKS


def in_column(b, y):
    x, _, z, c = coords(b)
    return block_at(x, y, z, c)


def kernel(
    e_hbm, partner_ref, prior_ref, grad_hbm, lse_ref,
    own, buf, scores, out, peak, total, lcol, pcol, lnb,
    load_sem, store_sem, s_up, s_dn, s_far, s_r9, s_r1, s_z, s_loc, s_lse, r_lse, recv,
):
    b = lax.axis_index("dp") * 8 + lax.axis_index("sub")
    x, y, z, c = coords(b)
    up, dn = block_at(x, (y + 1) % 4, z, c), block_at(x, (y + 3) % 4, z, c)
    mate = block_at(x, y, z, 1 - c)
    y0, y3 = y == 0, y == 3

    load = pltpu.make_async_copy(e_hbm, own, load_sem)
    load.start()

    barrier = pltpu.get_barrier_semaphore()

    def greet(t):
        pl.semaphore_signal(barrier, inc=1, device_id=device(t), device_id_type=MESH)

    for t in (up, dn, mate, near(b, 16 * c - 8)):
        greet(t)

    @pl.when(y0)
    def _():
        greet(in_column(near(b, -1), 0))
        greet(in_column(near(b, -9), 0))
        greet(in_column(near(b, -1), 0))
        greet(near(in_column(b, 3), 1))

    @pl.when(y3)
    def _():
        greet(in_column(near(b, 1), 3))
        greet(in_column(near(b, 9), 3))
        greet(in_column(near(b, 1), 3))
        greet(near(in_column(b, 0), -1))

    z_src = ((y == 1) & (c == 0)) | ((y == 2) & (c == 1))
    z_mid = ((y == 1) & (c == 1)) | ((y == 2) & (c == 0))

    @pl.when(z_mid)
    def _():
        greet(jnp.where(y == 1, near(in_column(b, 0), 9), near(in_column(b, 3), -9)))

    pl.semaphore_wait(barrier, 4 + jnp.where(y0 | y3, 4, 0) + jnp.where(z_src, 1, 0))

    up_dbl, up_sgl = y3 & (core(near(b, 1)) == 1), y3 & (core(near(b, 1)) == 0)
    dn_dbl, dn_sgl = y0 & (core(near(b, -1)) == 0), y0 & (core(near(b, -1)) == 1)
    q1 = jnp.where(y0, near(dn, 1), near(up, -1))
    q9 = jnp.where(y0, near(dn, 9), near(up, -9))
    wrap = y0 | y3
    rel_dbl = (y0 & (core(q1) == 1)) | (y3 & (core(q1) == 0))
    rel_sgl = wrap & ~rel_dbl
    rel_z = (y3 & (c == 0)) | (y0 & (c == 1))
    do_far = ((~y0) & (c == 1)) | ((~y3) & (c == 0))
    loc_late = (y0 & (c == 0)) | (y3 & (c == 1))
    near_slot, far_slot = jnp.where(y0, M1, P1), jnp.where(y0, M9, P9)

    def rows(k):
        return pl.ds(pl.multiple_of(k * R, R), R)

    def copy(src, to, slot, k, sem):
        return pltpu.make_async_remote_copy(
            src_ref=src, dst_ref=buf.at[slot, rows(k)], send_sem=sem, recv_sem=recv.at[slot, k],
            device_id=device(to), device_id_type=MESH,
        )

    def held(slot, k):
        return buf.at[slot, rows(k)]

    def arrived(slot, k):
        pltpu.make_async_copy(held(slot, k), held(slot, k), recv.at[slot, k]).wait()

    def send_up(k):
        odd = k % 2 == 1
        to = jnp.where(up_sgl & odd, in_column(near(b, 1), 3), up)
        slot = jnp.where(y3, jnp.where(up_sgl & odd, RZ, RL), M1)
        return copy(e_hbm.at[rows(k)], to, slot, k, s_up.at[k])

    def send_dn(k):
        odd = k % 2 == 1
        to = jnp.where(dn_sgl & odd, in_column(near(b, -1), 0), dn)
        slot = jnp.where(y0, jnp.where(dn_sgl & odd, RZ, RL), P1)
        return copy(e_hbm.at[rows(k)], to, slot, k, s_dn.at[k])

    def send_far(k):
        return copy(
            held(jnp.where(c == 1, M1, P1), k), jnp.where(c == 1, near(b, 8), near(b, -8)),
            jnp.where(c == 1, M9, P9), k, s_far.at[k],
        )

    def send_r1(k):
        return copy(held(RL, k), q1, near_slot, k, s_r1.at[k])

    def send_r9(k):
        return copy(held(RL, k), q9, far_slot, k, s_r9.at[k])

    def send_z(k):
        ahead = (y == 0) | (y == 1)
        slot = jnp.where(y3, M1, jnp.where(y0, P1, jnp.where(y == 1, P9, M9)))
        return copy(held(RZ, k), jnp.where(ahead, dn, up), slot, k, s_z.at[k])

    def send_side(k):
        to = jnp.where(y == 1, in_column(near(b, -9), 1), in_column(near(b, 9), 2))
        return copy(e_hbm.at[rows(k)], to, RZ, k, s_z.at[k])

    def send_loc(k):
        return copy(held(jnp.where(c == 0, M1, P1), k), mate, jnp.where(c == 0, M9, P9), k, s_loc.at[k])

    def z_moves(k):
        return (rel_z & (k % 2 == 1)) | (z_mid & (k % 4 == 3))

    def far_moves(k):
        return do_far & ~(wrap & (k % 4 == 3))

    def start_own(k):
        @pl.when(z_src & (k % 4 == 3))
        def _():
            send_side(k).start()

        send_up(k).start()
        send_dn(k).start()

    for k in range(AHEAD):
        start_own(k)

    def column(row):
        return jnp.transpose(jnp.broadcast_to(row, (128, ROWS)))

    def scored(left, right):
        return (SCALE * LOG2E) * lax.dot_general(
            left, right, (((1,), (1,)), ((), ())), preferred_element_type=jnp.float32
        )

    peak[...] = jnp.full((ROWS, 128), 10 * MASKED)
    total[...] = jnp.zeros((ROWS, 128), jnp.float32)

    def gather_stats(t, cols):
        def stats(r, carry):
            at = pl.ds(pl.multiple_of(r * 128, 128), 128)
            tile = scores[t, at, cols]
            old = peak[at, :]
            top = jnp.maximum(old, jnp.maximum(tile[:, :128], tile[:, 128:]))
            peak[at, :] = top
            total[at, :] = (
                total[at, :] * jnp.exp2(old - top) + jnp.exp2(tile[:, :128] - top) + jnp.exp2(tile[:, 128:] - top)
            )
            return carry

        lax.fori_loop(0, ROWS // 128, stats, 0, unroll=2)

    def step(k, carry):
        @pl.when(k + AHEAD < CHUNKS)
        def _():
            send_up(k).wait_send()
            send_dn(k).wait_send()
            start_own(k + AHEAD)

        @pl.when(k < CHUNKS)
        def _():
            odd = k % 2 == 1

            @pl.when(rel_dbl)
            def _():
                arrived(RL, k)
                send_r1(k).start()
                send_r9(k).start()

            @pl.when(rel_sgl & ~odd)
            def _():
                arrived(RL, k)
                send_r1(k).start()

            @pl.when(z_moves(k))
            def _():
                arrived(RZ, k)
                send_z(k).start()

            @pl.when(~y0)
            def _():
                arrived(M1, k)

            @pl.when(~y3)
            def _():
                arrived(P1, k)

            @pl.when(far_moves(k))
            def _():
                send_far(k).start()

            @pl.when(~loc_late)
            def _():
                send_loc(k).start()

        @pl.when((k >= LAG) & (k < CHUNKS + LAG))
        def _():
            j = k - LAG

            @pl.when(y0)
            def _():
                arrived(M1, j)

            @pl.when(y3)
            def _():
                arrived(P1, j)

            @pl.when(loc_late)
            def _():
                send_loc(j).start()

        @pl.when((k % PACE == 0) & (k < 4 * PACE))
        def _():
            g = k // PACE
            cols = pl.ds(pl.multiple_of(g * GROUP, GROUP), GROUP)
            tile = scored(own[...], own[cols, :])
            diagonal = lax.broadcasted_iota(jnp.int32, tile.shape, 0) == (
                lax.broadcasted_iota(jnp.int32, tile.shape, 1) + g * GROUP
            )
            scores[4, :, cols] = jnp.where(diagonal, MASKED, tile)
            gather_stats(4, cols)

        @pl.when((k % PACE == 0) & (k >= BEHIND))
        def _():
            item = (k - BEHIND) // PACE
            g, t = item // 4, item % 4

            @pl.when(t >= 2)
            def _():
                for i in range(PER_GROUP):
                    arrived(t, g * PER_GROUP + i)

            cols = pl.ds(pl.multiple_of(g * GROUP, GROUP), GROUP)
            scores[t, :, cols] = scored(own[...], buf[t, cols, :])
            gather_stats(t, cols)

        return carry

    load.wait()
    lax.fori_loop(0, CHUNKS + BEHIND, step, 0)

    prior = column(prior_ref[...] * LOG2E)
    lane_peak = peak[...]
    top = jnp.broadcast_to(jnp.max(lane_peak, axis=1, keepdims=True), (ROWS, 128))
    summed = jnp.sum(total[...] * jnp.exp2(lane_peak - top), axis=1, keepdims=True)
    both = jnp.maximum(top, prior)
    lse2 = both + jnp.log2(summed * jnp.exp2(top - both) + jnp.exp2(prior - both))
    lcol[...] = lse2
    lnb[4] = jnp.transpose(lse2)[0:8, :]
    lse_ref[...] = lnb[4, 0:1, :] * LN2

    def send_lse(t, to):
        return pltpu.make_async_remote_copy(
            src_ref=lnb.at[4], dst_ref=lnb.at[t], send_sem=s_lse.at[t], recv_sem=r_lse.at[t],
            device_id=device(to), device_id_type=MESH,
        )

    lse_sends = [send_lse(M1, near(b, 1)), send_lse(P1, near(b, -1)), send_lse(M9, near(b, 9)), send_lse(P9, near(b, -9))]
    for s in lse_sends:
        s.start()

    def weights(t, at):
        parts = []
        mine = lcol[at, :]
        for i in range(8):
            lanes = slice(i * 128, (i + 1) * 128)
            tile = scores[t, at, lanes]
            parts.append(jnp.exp2(tile - mine) + jnp.exp2(tile - lnb[t, 0:1, lanes]))
        return parts

    prow = (partner_ref[...] % ROWS).astype(jnp.float32)
    pcol[...] = column(prow)

    def own_part(r, carry):
        at = pl.ds(pl.multiple_of(r * 256, 256), 256)
        parts = weights(4, at)
        mine = pcol[at, :]
        row = (lax.broadcasted_iota(jnp.int32, (256, 128), 0) + r * 256).astype(jnp.float32)
        lane = lax.broadcasted_iota(jnp.int32, (256, 128), 1).astype(jnp.float32)
        for i in range(8):
            lanes = slice(i * 128, (i + 1) * 128)
            hot = jnp.where(mine == lane + i * 128.0, 1.0, 0.0) + jnp.where(prow[:, lanes] == row, 1.0, 0.0)
            parts[i] = (parts[i] - hot).astype(jnp.bfloat16)
        out[at, :] = jnp.dot(jnp.concatenate(parts, axis=1), own[...], preferred_element_type=jnp.float32)
        return carry

    lax.fori_loop(0, 4, own_part, 0)

    for s in lse_sends:
        s.wait_recv()

    def rest(r, carry):
        at = pl.ds(pl.multiple_of(r * 256, 256), 256)
        acc = out[at, :]
        for t in (P1, P9, M1, M9):
            w = jnp.concatenate([p.astype(jnp.bfloat16) for p in weights(t, at)], axis=1)
            term = jnp.dot(w, buf[t], preferred_element_type=jnp.float32)
            if t in (M1, M9):
                term = term.astype(jnp.bfloat16).astype(jnp.float32)
            acc = acc + term
        out[at, :] = SCALE * acc
        pltpu.make_async_copy(out.at[at], grad_hbm.at[at], store_sem.at[r]).start()
        return carry

    lax.fori_loop(0, 4, rest, 0)

    for s in lse_sends:
        s.wait_send()

    def sent(k, carry):
        odd = k % 2 == 1
        @pl.when(k + AHEAD >= CHUNKS)
        def _():
            send_up(k).wait_send()
            send_dn(k).wait_send()

        send_loc(k).wait_send()

        @pl.when(far_moves(k))
        def _():
            send_far(k).wait_send()

        @pl.when(rel_dbl)
        def _():
            send_r1(k).wait_send()
            send_r9(k).wait_send()

        @pl.when(rel_sgl & ~odd)
        def _():
            send_r1(k).wait_send()

        @pl.when(z_src & (k % 4 == 3))
        def _():
            send_side(k).wait_send()

        @pl.when(z_moves(k))
        def _():
            send_z(k).wait_send()

        return carry

    lax.fori_loop(0, CHUNKS, sent, 0)

    def stored(r, carry):
        at = pl.ds(pl.multiple_of(r * 256, 256), 256)
        pltpu.make_async_copy(out.at[at], grad_hbm.at[at], store_sem.at[r]).wait()
        return carry

    lax.fori_loop(0, 4, stored, 0)


def per_device(embeddings, partner, prior_lse):
    dma = pltpu.SemaphoreType.DMA
    f32 = jnp.float32
    gradient, lse = pl.pallas_call(
        kernel,
        out_shape=(pltpu.VMEM((ROWS, D), f32), jax.ShapeDtypeStruct((1, ROWS), f32)),
        in_specs=[
            pl.BlockSpec(memory_space=pl.ANY),
            pl.BlockSpec(memory_space=pltpu.VMEM),
            pl.BlockSpec(memory_space=pltpu.VMEM),
        ],
        out_specs=(pl.BlockSpec(memory_space=pl.ANY), pl.BlockSpec(memory_space=pltpu.VMEM)),
        scratch_shapes=[
            pltpu.VMEM((ROWS, D), jnp.bfloat16),
            pltpu.VMEM((6, ROWS, D), jnp.bfloat16),
            pltpu.VMEM((5, ROWS, ROWS), f32),
            pltpu.VMEM((ROWS, D), f32),
            pltpu.VMEM((ROWS, 128), f32),
            pltpu.VMEM((ROWS, 128), f32),
            pltpu.VMEM((ROWS, 128), f32),
            pltpu.VMEM((ROWS, 128), f32),
            pltpu.VMEM((5, 8, ROWS), f32),
            dma, dma((4,)), dma((CHUNKS,)), dma((CHUNKS,)), dma((CHUNKS,)), dma((CHUNKS,)), dma((CHUNKS,)),
            dma((CHUNKS,)), dma((CHUNKS,)), dma((4,)), dma((4,)), dma((6, CHUNKS)),
        ],
        compiler_params=pltpu.CompilerParams(collective_id=0, has_side_effects=True, vmem_limit_bytes=56 << 20),
        cost_estimate=pl.CostEstimate(flops=20 * ROWS * ROWS * D, bytes_accessed=8 << 20, transcendentals=20 << 20),
    )(embeddings, partner.reshape(1, ROWS), prior_lse.reshape(1, ROWS))
    return gradient, lse.reshape(ROWS)


def solution(mesh):
    placed = (P(("dp", "sub"), None), P(("dp", "sub")), P(("dp", "sub")))
    return jax.shard_map(
        per_device,
        mesh=mesh,
        in_specs=placed,
        out_specs=(P(("dp", "sub"), None), P(("dp", "sub"))),
        check_vma=False,
    )
```

```python
import functools
import math

import jax
import jax.numpy as jnp
from jax import lax
from jax.experimental import pallas as pl
from jax.experimental.pallas import tpu as pltpu
from jax.sharding import PartitionSpec as P

MESH = pl.DeviceIdType.MESH
BLOCKS = 128
ROWS = 1024
D = 1024
SCALE = 20.0
LOG2E = math.log2(math.e)
LN2 = math.log(2.0)
CHUNKS = 16
AHEAD = 4
PACE = CHUNKS // 16
R = ROWS // CHUNKS
GROUP = 256
PER_GROUP = GROUP // R
LAG = 2 * PACE
BEHIND = 5 * PACE
MASKED = -1e37
M1, P1, M9, P9, RL, RZ = range(6)


def coords(b):
    dp, sub = b // 8, b % 8
    return dp // 4, sub % 4, (dp // 2) % 2 * 2 + sub // 4, dp % 2


def block_at(x, y, z, c):
    return ((x * 2 + z // 2) * 2 + c) * 8 + (z % 2) * 4 + y


def device(b):
    return (b // 8, b % 8)


def core(b):
    return (b // 8) % 2


def near(b, step):
    return (b + BLOCKS + step) % BLOCKS


def in_column(b, y):
    x, _, z, c = coords(b)
    return block_at(x, y, z, c)


def aside(k):
    return (k % 4 == 3) | (k % 8 == 1)


def kernel(
    e_hbm, partner_ref, prior_ref, out, lse_ref,
    own, buf, scores, peak, total, lcol, pcol, lnb, packed,
    load_sem, s_up, s_dn, s_far, s_r9, s_r1, s_z, s_loc, s_lse, r_lse, recv,
):
    b = lax.axis_index("dp") * 8 + lax.axis_index("sub")
    x, y, z, c = coords(b)
    up, dn = block_at(x, (y + 1) % 4, z, c), block_at(x, (y + 3) % 4, z, c)
    mate = block_at(x, y, z, 1 - c)
    y0, y3 = y == 0, y == 3

    load = pltpu.make_async_copy(e_hbm, own, load_sem)
    load.start()

    barrier = pltpu.get_barrier_semaphore()

    def greet(t):
        pl.semaphore_signal(barrier, inc=1, device_id=device(t), device_id_type=MESH)

    for t in (up, dn, mate, near(b, 16 * c - 8)):
        greet(t)

    @pl.when(y0)
    def _():
        greet(in_column(near(b, -1), 0))
        greet(in_column(near(b, -9), 0))
        greet(in_column(near(b, -1), 0))
        greet(near(in_column(b, 3), 1))

    @pl.when(y3)
    def _():
        greet(in_column(near(b, 1), 3))
        greet(in_column(near(b, 9), 3))
        greet(in_column(near(b, 1), 3))
        greet(near(in_column(b, 0), -1))

    z_src = ((y == 1) & (c == 0)) | ((y == 2) & (c == 1))
    z_mid = ((y == 1) & (c == 1)) | ((y == 2) & (c == 0))

    @pl.when(z_mid)
    def _():
        greet(jnp.where(y == 1, near(in_column(b, 0), 9), near(in_column(b, 3), -9)))

    pl.semaphore_wait(barrier, 4 + jnp.where(y0 | y3, 4, 0) + jnp.where(z_src, 1, 0))

    up_dbl, up_sgl = y3 & (core(near(b, 1)) == 1), y3 & (core(near(b, 1)) == 0)
    dn_dbl, dn_sgl = y0 & (core(near(b, -1)) == 0), y0 & (core(near(b, -1)) == 1)
    q1 = jnp.where(y0, near(dn, 1), near(up, -1))
    q9 = jnp.where(y0, near(dn, 9), near(up, -9))
    wrap = y0 | y3
    rel_dbl = (y0 & (core(q1) == 1)) | (y3 & (core(q1) == 0))
    rel_sgl = wrap & ~rel_dbl
    rel_z = (y3 & (c == 0)) | (y0 & (c == 1))
    do_far = ((~y0) & (c == 1)) | ((~y3) & (c == 0))
    loc_late = (y0 & (c == 0)) | (y3 & (c == 1))
    near_slot, far_slot = jnp.where(y0, M1, P1), jnp.where(y0, M9, P9)

    def rows(k):
        return pl.ds(pl.multiple_of(k * R, R), R)

    def copy(src, to, slot, k, sem):
        return pltpu.make_async_remote_copy(
            src_ref=src, dst_ref=buf.at[slot, rows(k)], send_sem=sem, recv_sem=recv.at[slot, k],
            device_id=device(to), device_id_type=MESH,
        )

    def held(slot, k):
        return buf.at[slot, rows(k)]

    def arrived(slot, k):
        pltpu.make_async_copy(held(slot, k), held(slot, k), recv.at[slot, k]).wait()

    def send_up(k):
        odd = k % 2 == 1
        to = jnp.where(up_sgl & odd, in_column(near(b, 1), 3), up)
        slot = jnp.where(y3, jnp.where(up_sgl & odd, RZ, RL), M1)
        return copy(e_hbm.at[rows(k)], to, slot, k, s_up.at[k])

    def send_dn(k):
        odd = k % 2 == 1
        to = jnp.where(dn_sgl & odd, in_column(near(b, -1), 0), dn)
        slot = jnp.where(y0, jnp.where(dn_sgl & odd, RZ, RL), P1)
        return copy(e_hbm.at[rows(k)], to, slot, k, s_dn.at[k])

    def send_far(k):
        return copy(
            held(jnp.where(c == 1, M1, P1), k), jnp.where(c == 1, near(b, 8), near(b, -8)),
            jnp.where(c == 1, M9, P9), k, s_far.at[k],
        )

    def send_r1(k):
        return copy(held(RL, k), q1, near_slot, k, s_r1.at[k])

    def send_r9(k):
        return copy(held(RL, k), q9, far_slot, k, s_r9.at[k])

    def send_z(k):
        ahead = (y == 0) | (y == 1)
        slot = jnp.where(y3, M1, jnp.where(y0, P1, jnp.where(y == 1, P9, M9)))
        return copy(held(RZ, k), jnp.where(ahead, dn, up), slot, k, s_z.at[k])

    def send_side(k):
        to = jnp.where(y == 1, in_column(near(b, -9), 1), in_column(near(b, 9), 2))
        return copy(e_hbm.at[rows(k)], to, RZ, k, s_z.at[k])

    def send_loc(k):
        return copy(held(jnp.where(c == 0, M1, P1), k), mate, jnp.where(c == 0, M9, P9), k, s_loc.at[k])

    def z_moves(k):
        return (rel_z & (k % 2 == 1)) | (z_mid & aside(k))

    def far_moves(k):
        return do_far & ~(wrap & aside(k))

    def start_own(k):
        @pl.when(z_src & aside(k))
        def _():
            send_side(k).start()

        send_up(k).start()
        send_dn(k).start()

    for k in range(AHEAD):
        start_own(k)

    def column(row):
        return jnp.transpose(jnp.broadcast_to(row, (128, ROWS)))

    def scored(left, right):
        return (SCALE * LOG2E) * lax.dot_general(
            left, right, (((1,), (1,)), ((), ())), preferred_element_type=jnp.float32
        )

    peak[...] = jnp.full((ROWS, 128), 10 * MASKED)
    total[...] = jnp.zeros((ROWS, 128), jnp.float32)

    def gather_stats(t, cols):
        def stats(r, carry):
            at = pl.ds(pl.multiple_of(r * 128, 128), 128)
            tile = scores[t, at, cols]
            old = peak[at, :]
            top = jnp.maximum(old, jnp.maximum(tile[:, :128], tile[:, 128:]))
            peak[at, :] = top
            total[at, :] = (
                total[at, :] * jnp.exp2(old - top) + jnp.exp2(tile[:, :128] - top) + jnp.exp2(tile[:, 128:] - top)
            )
            return carry

        lax.fori_loop(0, ROWS // 128, stats, 0, unroll=2)

    def step(k, carry):
        @pl.when(k + AHEAD < CHUNKS)
        def _():
            send_up(k).wait_send()
            send_dn(k).wait_send()
            start_own(k + AHEAD)

        @pl.when(k < CHUNKS)
        def _():
            odd = k % 2 == 1

            @pl.when(rel_dbl)
            def _():
                arrived(RL, k)
                send_r1(k).start()
                send_r9(k).start()

            @pl.when(rel_sgl & ~odd)
            def _():
                arrived(RL, k)
                send_r1(k).start()

            @pl.when(z_moves(k))
            def _():
                arrived(RZ, k)
                send_z(k).start()

            @pl.when(~y0)
            def _():
                arrived(M1, k)

            @pl.when(~y3)
            def _():
                arrived(P1, k)

            @pl.when(far_moves(k))
            def _():
                send_far(k).start()

            @pl.when(~loc_late)
            def _():
                send_loc(k).start()

        @pl.when((k >= LAG) & (k < CHUNKS + LAG))
        def _():
            j = k - LAG

            @pl.when(y0)
            def _():
                arrived(M1, j)

            @pl.when(y3)
            def _():
                arrived(P1, j)

            @pl.when(loc_late)
            def _():
                send_loc(j).start()

        @pl.when((k % PACE == 0) & (k < 4 * PACE))
        def _():
            g = k // PACE
            cols = pl.ds(pl.multiple_of(g * GROUP, GROUP), GROUP)
            tile = scored(own[...], own[cols, :])
            diagonal = lax.broadcasted_iota(jnp.int32, tile.shape, 0) == (
                lax.broadcasted_iota(jnp.int32, tile.shape, 1) + g * GROUP
            )
            scores[4, :, cols] = jnp.where(diagonal, MASKED, tile)
            gather_stats(4, cols)

        @pl.when((k % PACE == 0) & (k >= BEHIND))
        def _():
            item = (k - BEHIND) // PACE
            g, t = item // 4, item % 4

            @pl.when(t >= 2)
            def _():
                for i in range(PER_GROUP):
                    arrived(t, g * PER_GROUP + i)

            cols = pl.ds(pl.multiple_of(g * GROUP, GROUP), GROUP)
            scores[t, :, cols] = scored(own[...], buf[t, cols, :])
            gather_stats(t, cols)

        return carry

    load.wait()
    lax.fori_loop(0, CHUNKS + BEHIND, step, 0)

    prior = column(prior_ref[...] * LOG2E)
    lane_peak = peak[...]
    top = jnp.broadcast_to(jnp.max(lane_peak, axis=1, keepdims=True), (ROWS, 128))
    summed = jnp.sum(total[...] * jnp.exp2(lane_peak - top), axis=1, keepdims=True)
    both = jnp.maximum(top, prior)
    lse2 = both + jnp.log2(summed * jnp.exp2(top - both) + jnp.exp2(prior - both))
    row = jnp.transpose(lse2)[0:1, :]
    for i in range(8):
        packed[4, i : i + 1, :] = row[:, i * 128 : (i + 1) * 128]

    def send_lse(t, to):
        return pltpu.make_async_remote_copy(
            src_ref=packed.at[4], dst_ref=packed.at[t], send_sem=s_lse.at[t], recv_sem=r_lse.at[t],
            device_id=device(to), device_id_type=MESH,
        )

    lse_sends = [send_lse(M1, near(b, 1)), send_lse(P1, near(b, -1)), send_lse(M9, near(b, 9)), send_lse(P9, near(b, -9))]
    for s in lse_sends:
        s.start()
    lcol[...] = lse2
    lnb[4, 0:1, :] = row
    lse_ref[...] = row * LN2

    def weights(t, at):
        parts = []
        mine = lcol[at, :]
        for i in range(8):
            lanes = slice(i * 128, (i + 1) * 128)
            tile = scores[t, at, lanes]
            parts.append(jnp.exp2(tile - mine) + jnp.exp2(tile - lnb[t, 0:1, lanes]))
        return parts

    prow = (partner_ref[...] % ROWS).astype(jnp.float32)
    pcol[...] = column(prow)

    def own_part(r, carry):
        at = pl.ds(pl.multiple_of(r * 512, 512), 512)
        parts = weights(4, at)
        mine = pcol[at, :]
        row = (lax.broadcasted_iota(jnp.int32, (512, 128), 0) + r * 512).astype(jnp.float32)
        lane = lax.broadcasted_iota(jnp.int32, (512, 128), 1).astype(jnp.float32)
        for i in range(8):
            lanes = slice(i * 128, (i + 1) * 128)
            hot = jnp.where(mine == lane + i * 128.0, 1.0, 0.0) + jnp.where(prow[:, lanes] == row, 1.0, 0.0)
            parts[i] = (parts[i] - hot).astype(jnp.bfloat16)
        out[at, :] = jnp.dot(jnp.concatenate(parts, axis=1), own[...], preferred_element_type=jnp.float32)
        return carry

    lax.fori_loop(0, 2, own_part, 0)

    order = (P1, M1, P9, M9)
    for t in order:
        lse_sends[t].wait_recv()
        for i in range(8):
            lnb[t, 0:1, i * 128 : (i + 1) * 128] = packed[t, i : i + 1, :]

        def term(r, carry):
            at = pl.ds(pl.multiple_of(r * 512, 512), 512)
            w = jnp.concatenate([p.astype(jnp.bfloat16) for p in weights(t, at)], axis=1)
            part = jnp.dot(w, buf[t], preferred_element_type=jnp.float32)
            if t in (M1, M9):
                part = part.astype(jnp.bfloat16).astype(jnp.float32)
            acc = out[at, :] + part
            out[at, :] = SCALE * acc if t == order[-1] else acc
            return carry

        lax.fori_loop(0, ROWS // 512, term, 0)

    for s in lse_sends:
        s.wait_send()

    def sent(k, carry):
        odd = k % 2 == 1
        @pl.when(k + AHEAD >= CHUNKS)
        def _():
            send_up(k).wait_send()
            send_dn(k).wait_send()

        send_loc(k).wait_send()

        @pl.when(far_moves(k))
        def _():
            send_far(k).wait_send()

        @pl.when(rel_dbl)
        def _():
            send_r1(k).wait_send()
            send_r9(k).wait_send()

        @pl.when(rel_sgl & ~odd)
        def _():
            send_r1(k).wait_send()

        @pl.when(z_src & aside(k))
        def _():
            send_side(k).wait_send()

        @pl.when(z_moves(k))
        def _():
            send_z(k).wait_send()

        return carry

    lax.fori_loop(0, CHUNKS, sent, 0)


def per_device(embeddings, partner, prior_lse):
    dma = pltpu.SemaphoreType.DMA
    f32 = jnp.float32
    gradient, lse = pl.pallas_call(
        kernel,
        out_shape=(pltpu.VMEM((ROWS, D), f32), jax.ShapeDtypeStruct((1, ROWS), f32)),
        in_specs=[
            pl.BlockSpec(memory_space=pltpu.HBM),
            pl.BlockSpec(memory_space=pltpu.VMEM),
            pl.BlockSpec(memory_space=pltpu.VMEM),
        ],
        out_specs=(pl.BlockSpec(memory_space=pltpu.VMEM), pl.BlockSpec(memory_space=pltpu.VMEM)),
        scratch_shapes=[
            pltpu.VMEM((ROWS, D), jnp.bfloat16),
            pltpu.VMEM((6, ROWS, D), jnp.bfloat16),
            pltpu.VMEM((5, ROWS, ROWS), f32),
            pltpu.VMEM((ROWS, 128), f32),
            pltpu.VMEM((ROWS, 128), f32),
            pltpu.VMEM((ROWS, 128), f32),
            pltpu.VMEM((ROWS, 128), f32),
            pltpu.VMEM((5, 8, ROWS), f32),
            pltpu.VMEM((5, 8, 128), f32),
            dma, dma((CHUNKS,)), dma((CHUNKS,)), dma((CHUNKS,)), dma((CHUNKS,)), dma((CHUNKS,)),
            dma((CHUNKS,)), dma((CHUNKS,)), dma((4,)), dma((4,)), dma((6, CHUNKS)),
        ],
        compiler_params=pltpu.CompilerParams(collective_id=0, has_side_effects=True, vmem_limit_bytes=56 << 20),
        cost_estimate=pl.CostEstimate(flops=20 * ROWS * ROWS * D, bytes_accessed=8 << 20, transcendentals=20 << 20),
    )(embeddings, partner.reshape(1, ROWS), prior_lse.reshape(1, ROWS))
    return gradient, lse.reshape(ROWS)


def solution(mesh):
    placed = (P(("dp", "sub"), None), P(("dp", "sub")), P(("dp", "sub")))
    return jax.shard_map(
        per_device,
        mesh=mesh,
        in_specs=placed,
        out_specs=(P(("dp", "sub"), None), P(("dp", "sub"))),
        check_vma=False,
    )
```

```python
import functools
import math

import jax
import jax.numpy as jnp
from jax import lax
from jax.experimental import pallas as pl
from jax.experimental.pallas import tpu as pltpu
from jax.sharding import PartitionSpec as P

MESH = pl.DeviceIdType.MESH
BLOCKS = 128
ROWS = 1024
D = 1024
SCALE = 20.0
LOG2E = math.log2(math.e)
LN2 = math.log(2.0)
CHUNKS = 16
AHEAD = 4
PACE = CHUNKS // 16
R = ROWS // CHUNKS
GROUP = 256
PER_GROUP = GROUP // R
LAG = 2 * PACE
BEHIND = 5 * PACE
MASKED = -1e37
M1, P1, M9, P9, RL, RZ = range(6)


def coords(b):
    dp, sub = b // 8, b % 8
    return dp // 4, sub % 4, (dp // 2) % 2 * 2 + sub // 4, dp % 2


def block_at(x, y, z, c):
    return ((x * 2 + z // 2) * 2 + c) * 8 + (z % 2) * 4 + y


def device(b):
    return (b // 8, b % 8)


def core(b):
    return (b // 8) % 2


def near(b, step):
    return (b + BLOCKS + step) % BLOCKS


def in_column(b, y):
    x, _, z, c = coords(b)
    return block_at(x, y, z, c)


def aside(k):
    return (k % 4 == 3) | (k % 8 == 1)


def by_z(k):
    return (k % 2 == 1) | (k % 8 == 4)


def kernel(
    e_hbm, partner_ref, prior_ref, out, lse_ref,
    own, buf, scores, peak, total, lcol, pcol, lnb, packed,
    load_sem, s_up, s_dn, s_far, s_r9, s_r1, s_z, s_loc, s_lse, r_lse, recv,
):
    b = lax.axis_index("dp") * 8 + lax.axis_index("sub")
    x, y, z, c = coords(b)
    up, dn = block_at(x, (y + 1) % 4, z, c), block_at(x, (y + 3) % 4, z, c)
    mate = block_at(x, y, z, 1 - c)
    y0, y3 = y == 0, y == 3

    load = pltpu.make_async_copy(e_hbm, own, load_sem)
    load.start()

    barrier = pltpu.get_barrier_semaphore()

    def greet(t):
        pl.semaphore_signal(barrier, inc=1, device_id=device(t), device_id_type=MESH)

    for t in (up, dn, mate, near(b, 16 * c - 8)):
        greet(t)

    @pl.when(y0)
    def _():
        greet(in_column(near(b, -1), 0))
        greet(in_column(near(b, -9), 0))
        greet(in_column(near(b, -1), 0))
        greet(near(in_column(b, 3), 1))

    @pl.when(y3)
    def _():
        greet(in_column(near(b, 1), 3))
        greet(in_column(near(b, 9), 3))
        greet(in_column(near(b, 1), 3))
        greet(near(in_column(b, 0), -1))

    z_src = ((y == 1) & (c == 0)) | ((y == 2) & (c == 1))
    z_mid = ((y == 1) & (c == 1)) | ((y == 2) & (c == 0))

    @pl.when(z_mid)
    def _():
        greet(jnp.where(y == 1, near(in_column(b, 0), 9), near(in_column(b, 3), -9)))

    pl.semaphore_wait(barrier, 4 + jnp.where(y0 | y3, 4, 0) + jnp.where(z_src, 1, 0))

    up_dbl, up_sgl = y3 & (core(near(b, 1)) == 1), y3 & (core(near(b, 1)) == 0)
    dn_dbl, dn_sgl = y0 & (core(near(b, -1)) == 0), y0 & (core(near(b, -1)) == 1)
    q1 = jnp.where(y0, near(dn, 1), near(up, -1))
    q9 = jnp.where(y0, near(dn, 9), near(up, -9))
    wrap = y0 | y3
    rel_dbl = (y0 & (core(q1) == 1)) | (y3 & (core(q1) == 0))
    rel_sgl = wrap & ~rel_dbl
    rel_z = (y3 & (c == 0)) | (y0 & (c == 1))
    do_far = ((~y0) & (c == 1)) | ((~y3) & (c == 0))
    loc_late = (y0 & (c == 0)) | (y3 & (c == 1))
    near_slot, far_slot = jnp.where(y0, M1, P1), jnp.where(y0, M9, P9)

    def rows(k):
        return pl.ds(pl.multiple_of(k * R, R), R)

    def copy(src, to, slot, k, sem):
        return pltpu.make_async_remote_copy(
            src_ref=src, dst_ref=buf.at[slot, rows(k)], send_sem=sem, recv_sem=recv.at[slot, k],
            device_id=device(to), device_id_type=MESH,
        )

    def held(slot, k):
        return buf.at[slot, rows(k)]

    def arrived(slot, k):
        pltpu.make_async_copy(held(slot, k), held(slot, k), recv.at[slot, k]).wait()

    def send_up(k):
        odd = by_z(k)
        to = jnp.where(up_sgl & odd, in_column(near(b, 1), 3), up)
        slot = jnp.where(y3, jnp.where(up_sgl & odd, RZ, RL), M1)
        return copy(e_hbm.at[rows(k)], to, slot, k, s_up.at[k])

    def send_dn(k):
        odd = by_z(k)
        to = jnp.where(dn_sgl & odd, in_column(near(b, -1), 0), dn)
        slot = jnp.where(y0, jnp.where(dn_sgl & odd, RZ, RL), P1)
        return copy(e_hbm.at[rows(k)], to, slot, k, s_dn.at[k])

    def send_far(k):
        return copy(
            held(jnp.where(c == 1, M1, P1), k), jnp.where(c == 1, near(b, 8), near(b, -8)),
            jnp.where(c == 1, M9, P9), k, s_far.at[k],
        )

    def send_r1(k):
        return copy(held(RL, k), q1, near_slot, k, s_r1.at[k])

    def send_r9(k):
        return copy(held(RL, k), q9, far_slot, k, s_r9.at[k])

    def send_z(k):
        ahead = (y == 0) | (y == 1)
        slot = jnp.where(y3, M1, jnp.where(y0, P1, jnp.where(y == 1, P9, M9)))
        return copy(held(RZ, k), jnp.where(ahead, dn, up), slot, k, s_z.at[k])

    def send_side(k):
        to = jnp.where(y == 1, in_column(near(b, -9), 1), in_column(near(b, 9), 2))
        return copy(e_hbm.at[rows(k)], to, RZ, k, s_z.at[k])

    def send_loc(k):
        return copy(held(jnp.where(c == 0, M1, P1), k), mate, jnp.where(c == 0, M9, P9), k, s_loc.at[k])

    def z_moves(k):
        return (rel_z & by_z(k)) | (z_mid & aside(k))

    def far_moves(k):
        return do_far & ~(wrap & aside(k))

    def start_own(k):
        @pl.when(z_src & aside(k))
        def _():
            send_side(k).start()

        send_up(k).start()
        send_dn(k).start()

    for k in range(AHEAD):
        start_own(k)

    def column(row):
        return jnp.transpose(jnp.broadcast_to(row, (128, ROWS)))

    def scored(left, right):
        return (SCALE * LOG2E) * lax.dot_general(
            left, right, (((1,), (1,)), ((), ())), preferred_element_type=jnp.float32
        )

    peak[...] = jnp.full((ROWS, 128), 10 * MASKED)
    total[...] = jnp.zeros((ROWS, 128), jnp.float32)

    def gather_stats(t, cols):
        def stats(r, carry):
            at = pl.ds(pl.multiple_of(r * 128, 128), 128)
            tile = scores[t, at, cols]
            old = peak[at, :]
            top = jnp.maximum(old, jnp.maximum(tile[:, :128], tile[:, 128:]))
            peak[at, :] = top
            total[at, :] = (
                total[at, :] * jnp.exp2(old - top) + jnp.exp2(tile[:, :128] - top) + jnp.exp2(tile[:, 128:] - top)
            )
            return carry

        lax.fori_loop(0, ROWS // 128, stats, 0, unroll=2)

    def step(k, carry):
        @pl.when(k + AHEAD < CHUNKS)
        def _():
            send_up(k).wait_send()
            send_dn(k).wait_send()
            start_own(k + AHEAD)

        @pl.when(k < CHUNKS)
        def _():
            odd = by_z(k)

            @pl.when(rel_dbl)
            def _():
                arrived(RL, k)
                send_r1(k).start()
                send_r9(k).start()

            @pl.when(rel_sgl & ~odd)
            def _():
                arrived(RL, k)
                send_r1(k).start()

            @pl.when(z_moves(k))
            def _():
                arrived(RZ, k)
                send_z(k).start()

            @pl.when(~y0)
            def _():
                arrived(M1, k)

            @pl.when(~y3)
            def _():
                arrived(P1, k)

            @pl.when(far_moves(k))
            def _():
                send_far(k).start()

            @pl.when(~loc_late)
            def _():
                send_loc(k).start()

        @pl.when((k >= LAG) & (k < CHUNKS + LAG))
        def _():
            j = k - LAG

            @pl.when(y0)
            def _():
                arrived(M1, j)

            @pl.when(y3)
            def _():
                arrived(P1, j)

            @pl.when(loc_late)
            def _():
                send_loc(j).start()

        @pl.when((k % PACE == 0) & (k < 4 * PACE))
        def _():
            g = k // PACE
            cols = pl.ds(pl.multiple_of(g * GROUP, GROUP), GROUP)
            tile = scored(own[...], own[cols, :])
            diagonal = lax.broadcasted_iota(jnp.int32, tile.shape, 0) == (
                lax.broadcasted_iota(jnp.int32, tile.shape, 1) + g * GROUP
            )
            scores[4, :, cols] = jnp.where(diagonal, MASKED, tile)
            gather_stats(4, cols)

        @pl.when((k % PACE == 0) & (k >= BEHIND))
        def _():
            item = (k - BEHIND) // PACE
            g, t = item // 4, item % 4

            @pl.when(t >= 2)
            def _():
                for i in range(PER_GROUP):
                    arrived(t, g * PER_GROUP + i)

            cols = pl.ds(pl.multiple_of(g * GROUP, GROUP), GROUP)
            scores[t, :, cols] = scored(own[...], buf[t, cols, :])
            gather_stats(t, cols)

        return carry

    load.wait()
    lax.fori_loop(0, CHUNKS + BEHIND, step, 0)

    prior = column(prior_ref[...] * LOG2E)
    lane_peak = peak[...]
    top = jnp.broadcast_to(jnp.max(lane_peak, axis=1, keepdims=True), (ROWS, 128))
    summed = jnp.sum(total[...] * jnp.exp2(lane_peak - top), axis=1, keepdims=True)
    both = jnp.maximum(top, prior)
    lse2 = both + jnp.log2(summed * jnp.exp2(top - both) + jnp.exp2(prior - both))
    row = jnp.transpose(lse2)[0:1, :]
    for i in range(8):
        packed[4, i : i + 1, :] = row[:, i * 128 : (i + 1) * 128]

    def send_lse(t, to):
        return pltpu.make_async_remote_copy(
            src_ref=packed.at[4], dst_ref=packed.at[t], send_sem=s_lse.at[t], recv_sem=r_lse.at[t],
            device_id=device(to), device_id_type=MESH,
        )

    lse_sends = [send_lse(M1, near(b, 1)), send_lse(P1, near(b, -1)), send_lse(M9, near(b, 9)), send_lse(P9, near(b, -9))]
    for s in lse_sends:
        s.start()
    lcol[...] = lse2
    lnb[4, 0:1, :] = row
    lse_ref[...] = row * LN2

    def weights(t, at):
        parts = []
        mine = lcol[at, :]
        for i in range(8):
            lanes = slice(i * 128, (i + 1) * 128)
            tile = scores[t, at, lanes]
            parts.append(jnp.exp2(tile - mine) + jnp.exp2(tile - lnb[t, 0:1, lanes]))
        return parts

    prow = (partner_ref[...] % ROWS).astype(jnp.float32)
    pcol[...] = column(prow)

    def own_part(r, carry):
        at = pl.ds(pl.multiple_of(r * 512, 512), 512)
        parts = weights(4, at)
        mine = pcol[at, :]
        row = (lax.broadcasted_iota(jnp.int32, (512, 128), 0) + r * 512).astype(jnp.float32)
        lane = lax.broadcasted_iota(jnp.int32, (512, 128), 1).astype(jnp.float32)
        for i in range(8):
            lanes = slice(i * 128, (i + 1) * 128)
            hot = jnp.where(mine == lane + i * 128.0, 1.0, 0.0) + jnp.where(prow[:, lanes] == row, 1.0, 0.0)
            parts[i] = (parts[i] - hot).astype(jnp.bfloat16)
        out[at, :] = jnp.dot(jnp.concatenate(parts, axis=1), own[...], preferred_element_type=jnp.float32)
        return carry

    lax.fori_loop(0, 2, own_part, 0)

    def sent(k, carry):
        odd = by_z(k)
        @pl.when(k + AHEAD >= CHUNKS)
        def _():
            send_up(k).wait_send()
            send_dn(k).wait_send()

        send_loc(k).wait_send()

        @pl.when(far_moves(k))
        def _():
            send_far(k).wait_send()

        @pl.when(rel_dbl)
        def _():
            send_r1(k).wait_send()
            send_r9(k).wait_send()

        @pl.when(rel_sgl & ~odd)
        def _():
            send_r1(k).wait_send()

        @pl.when(z_src & aside(k))
        def _():
            send_side(k).wait_send()

        @pl.when(z_moves(k))
        def _():
            send_z(k).wait_send()

        return carry

    lax.fori_loop(0, CHUNKS, sent, 0)

    order = (P1, M1, P9, M9)
    for t in order:
        lse_sends[t].wait_recv()
        for i in range(8):
            lnb[t, 0:1, i * 128 : (i + 1) * 128] = packed[t, i : i + 1, :]

        def term(r, carry):
            at = pl.ds(pl.multiple_of(r * 512, 512), 512)
            w = jnp.concatenate([p.astype(jnp.bfloat16) for p in weights(t, at)], axis=1)
            part = jnp.dot(w, buf[t], preferred_element_type=jnp.float32)
            if t in (M1, M9):
                part = part.astype(jnp.bfloat16).astype(jnp.float32)
            acc = out[at, :] + part
            out[at, :] = SCALE * acc if t == order[-1] else acc
            return carry

        lax.fori_loop(0, ROWS // 512, term, 0, unroll=True)

    for s in lse_sends:
        s.wait_send()


def per_device(embeddings, partner, prior_lse):
    dma = pltpu.SemaphoreType.DMA
    f32 = jnp.float32
    gradient, lse = pl.pallas_call(
        kernel,
        out_shape=(pltpu.VMEM((ROWS, D), f32), jax.ShapeDtypeStruct((1, ROWS), f32)),
        in_specs=[
            pl.BlockSpec(memory_space=pltpu.HBM),
            pl.BlockSpec(memory_space=pltpu.VMEM),
            pl.BlockSpec(memory_space=pltpu.VMEM),
        ],
        out_specs=(pl.BlockSpec(memory_space=pltpu.VMEM), pl.BlockSpec(memory_space=pltpu.VMEM)),
        scratch_shapes=[
            pltpu.VMEM((ROWS, D), jnp.bfloat16),
            pltpu.VMEM((6, ROWS, D), jnp.bfloat16),
            pltpu.VMEM((5, ROWS, ROWS), f32),
            pltpu.VMEM((ROWS, 128), f32),
            pltpu.VMEM((ROWS, 128), f32),
            pltpu.VMEM((ROWS, 128), f32),
            pltpu.VMEM((ROWS, 128), f32),
            pltpu.VMEM((5, 8, ROWS), f32),
            pltpu.VMEM((5, 8, 128), f32),
            dma, dma((CHUNKS,)), dma((CHUNKS,)), dma((CHUNKS,)), dma((CHUNKS,)), dma((CHUNKS,)),
            dma((CHUNKS,)), dma((CHUNKS,)), dma((4,)), dma((4,)), dma((6, CHUNKS)),
        ],
        compiler_params=pltpu.CompilerParams(collective_id=0, has_side_effects=True, vmem_limit_bytes=56 << 20),
        cost_estimate=pl.CostEstimate(flops=20 * ROWS * ROWS * D, bytes_accessed=8 << 20, transcendentals=20 << 20),
    )(embeddings, partner.reshape(1, ROWS), prior_lse.reshape(1, ROWS))
    return gradient, lse.reshape(ROWS)


def solution(mesh):
    placed = (P(("dp", "sub"), None), P(("dp", "sub")), P(("dp", "sub")))
    return jax.shard_map(
        per_device,
        mesh=mesh,
        in_specs=placed,
        out_specs=(P(("dp", "sub"), None), P(("dp", "sub"))),
        check_vma=False,
    )
```

```python
import functools
import math

import jax
import jax.numpy as jnp
from jax import lax
from jax.experimental import pallas as pl
from jax.experimental.pallas import tpu as pltpu
from jax.sharding import PartitionSpec as P

MESH = pl.DeviceIdType.MESH
BLOCKS = 128
ROWS = 1024
D = 1024
SCALE = 20.0
LOG2E = math.log2(math.e)
LN2 = math.log(2.0)
CHUNKS = 16
AHEAD = 4
PACE = CHUNKS // 16
R = ROWS // CHUNKS
GROUP = 256
PER_GROUP = GROUP // R
LAG = 2 * PACE
BEHIND = 5 * PACE
MASKED = -1e37
M1, P1, M9, P9, RL, RZ = range(6)


def coords(b):
    dp, sub = b // 8, b % 8
    return dp // 4, sub % 4, (dp // 2) % 2 * 2 + sub // 4, dp % 2


def block_at(x, y, z, c):
    return ((x * 2 + z // 2) * 2 + c) * 8 + (z % 2) * 4 + y


def device(b):
    return (b // 8, b % 8)


def core(b):
    return (b // 8) % 2


def near(b, step):
    return (b + BLOCKS + step) % BLOCKS


def in_column(b, y):
    x, _, z, c = coords(b)
    return block_at(x, y, z, c)


def aside(k):
    return (k % 4 == 3) | (k % 8 == 1)


def by_z(k):
    return (k % 2 == 1) | (k % 8 == 4)


def kernel(
    e_hbm, partner_ref, prior_ref, out, lse_ref,
    own, buf, scores, peak, total, lcol, pcol, lnb, packed,
    load_sem, s_up, s_dn, s_far, s_r9, s_r1, s_z, s_loc, s_lse, r_lse, recv,
):
    b = lax.axis_index("dp") * 8 + lax.axis_index("sub")
    x, y, z, c = coords(b)
    up, dn = block_at(x, (y + 1) % 4, z, c), block_at(x, (y + 3) % 4, z, c)
    mate = block_at(x, y, z, 1 - c)
    y0, y3 = y == 0, y == 3

    load = pltpu.make_async_copy(e_hbm, own, load_sem)
    load.start()

    barrier = pltpu.get_barrier_semaphore()

    def greet(t):
        pl.semaphore_signal(barrier, inc=1, device_id=device(t), device_id_type=MESH)

    for t in (up, dn, mate, near(b, 16 * c - 8)):
        greet(t)

    @pl.when(y0)
    def _():
        greet(in_column(near(b, -1), 0))
        greet(in_column(near(b, -9), 0))
        greet(in_column(near(b, -1), 0))
        greet(near(in_column(b, 3), 1))

    @pl.when(y3)
    def _():
        greet(in_column(near(b, 1), 3))
        greet(in_column(near(b, 9), 3))
        greet(in_column(near(b, 1), 3))
        greet(near(in_column(b, 0), -1))

    z_src = ((y == 1) & (c == 0)) | ((y == 2) & (c == 1))
    z_mid = ((y == 1) & (c == 1)) | ((y == 2) & (c == 0))

    @pl.when(z_mid)
    def _():
        greet(jnp.where(y == 1, near(in_column(b, 0), 9), near(in_column(b, 3), -9)))

    pl.semaphore_wait(barrier, 4 + jnp.where(y0 | y3, 4, 0) + jnp.where(z_src, 1, 0))

    up_dbl, up_sgl = y3 & (core(near(b, 1)) == 1), y3 & (core(near(b, 1)) == 0)
    dn_dbl, dn_sgl = y0 & (core(near(b, -1)) == 0), y0 & (core(near(b, -1)) == 1)
    q1 = jnp.where(y0, near(dn, 1), near(up, -1))
    q9 = jnp.where(y0, near(dn, 9), near(up, -9))
    wrap = y0 | y3
    rel_dbl = (y0 & (core(q1) == 1)) | (y3 & (core(q1) == 0))
    rel_sgl = wrap & ~rel_dbl
    rel_z = (y3 & (c == 0)) | (y0 & (c == 1))
    do_far = ((~y0) & (c == 1)) | ((~y3) & (c == 0))
    loc_late = (y0 & (c == 0)) | (y3 & (c == 1))
    near_slot, far_slot = jnp.where(y0, M1, P1), jnp.where(y0, M9, P9)

    def rows(k):
        return pl.ds(pl.multiple_of(k * R, R), R)

    def copy(src, to, slot, k, sem):
        return pltpu.make_async_remote_copy(
            src_ref=src, dst_ref=buf.at[slot, rows(k)], send_sem=sem, recv_sem=recv.at[slot, k],
            device_id=device(to), device_id_type=MESH,
        )

    def held(slot, k):
        return buf.at[slot, rows(k)]

    def arrived(slot, k):
        pltpu.make_async_copy(held(slot, k), held(slot, k), recv.at[slot, k]).wait()

    def send_up(k):
        odd = by_z(k)
        to = jnp.where(up_sgl & odd, in_column(near(b, 1), 3), up)
        slot = jnp.where(y3, jnp.where(up_sgl & odd, RZ, RL), M1)
        return copy(e_hbm.at[rows(k)], to, slot, k, s_up.at[k])

    def send_dn(k):
        odd = by_z(k)
        to = jnp.where(dn_sgl & odd, in_column(near(b, -1), 0), dn)
        slot = jnp.where(y0, jnp.where(dn_sgl & odd, RZ, RL), P1)
        return copy(e_hbm.at[rows(k)], to, slot, k, s_dn.at[k])

    def send_far(k):
        return copy(
            held(jnp.where(c == 1, M1, P1), k), jnp.where(c == 1, near(b, 8), near(b, -8)),
            jnp.where(c == 1, M9, P9), k, s_far.at[k],
        )

    def send_r1(k):
        return copy(held(RL, k), q1, near_slot, k, s_r1.at[k])

    def send_r9(k):
        return copy(held(RL, k), q9, far_slot, k, s_r9.at[k])

    def send_z(k):
        ahead = (y == 0) | (y == 1)
        slot = jnp.where(y3, M1, jnp.where(y0, P1, jnp.where(y == 1, P9, M9)))
        return copy(held(RZ, k), jnp.where(ahead, dn, up), slot, k, s_z.at[k])

    def send_side(k):
        to = jnp.where(y == 1, in_column(near(b, -9), 1), in_column(near(b, 9), 2))
        return copy(e_hbm.at[rows(k)], to, RZ, k, s_z.at[k])

    def send_loc(k):
        return copy(held(jnp.where(c == 0, M1, P1), k), mate, jnp.where(c == 0, M9, P9), k, s_loc.at[k])

    def z_moves(k):
        return (rel_z & by_z(k)) | (z_mid & aside(k))

    def far_moves(k):
        return do_far & ~(wrap & aside(k))

    def start_own(k):
        @pl.when(z_src & aside(k))
        def _():
            send_side(k).start()

        send_up(k).start()
        send_dn(k).start()

    for k in range(AHEAD):
        start_own(k)

    def column(row):
        return jnp.transpose(jnp.broadcast_to(row, (128, ROWS)))

    def scored(left, right):
        return (SCALE * LOG2E) * lax.dot_general(
            left, right, (((1,), (1,)), ((), ())), preferred_element_type=jnp.float32
        )

    peak[...] = jnp.full((ROWS, 128), 10 * MASKED)
    total[...] = jnp.zeros((ROWS, 128), jnp.float32)

    def gather_stats(t, cols):
        def stats(r, carry):
            at = pl.ds(pl.multiple_of(r * 128, 128), 128)
            tile = scores[t, at, cols]
            old = peak[at, :]
            top = jnp.maximum(old, jnp.maximum(tile[:, :128], tile[:, 128:]))
            peak[at, :] = top
            total[at, :] = (
                total[at, :] * jnp.exp2(old - top) + jnp.exp2(tile[:, :128] - top) + jnp.exp2(tile[:, 128:] - top)
            )
            return carry

        lax.fori_loop(0, ROWS // 128, stats, 0, unroll=2)

    def step(k, carry):
        @pl.when(k + AHEAD < CHUNKS)
        def _():
            send_up(k).wait_send()
            send_dn(k).wait_send()
            start_own(k + AHEAD)

        @pl.when(k < CHUNKS)
        def _():
            odd = by_z(k)

            @pl.when(rel_dbl)
            def _():
                arrived(RL, k)
                send_r1(k).start()
                send_r9(k).start()

            @pl.when(rel_sgl & ~odd)
            def _():
                arrived(RL, k)
                send_r1(k).start()

            @pl.when(z_moves(k))
            def _():
                arrived(RZ, k)
                send_z(k).start()

            @pl.when(~y0)
            def _():
                arrived(M1, k)

            @pl.when(~y3)
            def _():
                arrived(P1, k)

            @pl.when(far_moves(k))
            def _():
                send_far(k).start()

            @pl.when(~loc_late)
            def _():
                send_loc(k).start()

        @pl.when((k >= LAG) & (k < CHUNKS + LAG))
        def _():
            j = k - LAG

            @pl.when(y0)
            def _():
                arrived(M1, j)

            @pl.when(y3)
            def _():
                arrived(P1, j)

            @pl.when(loc_late)
            def _():
                send_loc(j).start()

        @pl.when((k % PACE == 0) & (k < 4 * PACE))
        def _():
            g = k // PACE
            cols = pl.ds(pl.multiple_of(g * GROUP, GROUP), GROUP)
            tile = scored(own[...], own[cols, :])
            diagonal = lax.broadcasted_iota(jnp.int32, tile.shape, 0) == (
                lax.broadcasted_iota(jnp.int32, tile.shape, 1) + g * GROUP
            )
            scores[4, :, cols] = jnp.where(diagonal, MASKED, tile)
            gather_stats(4, cols)

        @pl.when((k % PACE == 0) & (k >= BEHIND))
        def _():
            item = (k - BEHIND) // PACE
            g, t = item // 4, item % 4

            @pl.when(t >= 2)
            def _():
                for i in range(PER_GROUP):
                    arrived(t, g * PER_GROUP + i)

            cols = pl.ds(pl.multiple_of(g * GROUP, GROUP), GROUP)
            scores[t, :, cols] = scored(own[...], buf[t, cols, :])
            gather_stats(t, cols)

        return carry

    lcol[...] = column(prior_ref[...] * LOG2E)
    load.wait()
    lax.fori_loop(0, CHUNKS + BEHIND, step, 0)

    prior = lcol[...]
    lane_peak = peak[...]
    top = jnp.broadcast_to(jnp.max(lane_peak, axis=1, keepdims=True), (ROWS, 128))
    summed = jnp.sum(total[...] * jnp.exp2(lane_peak - top), axis=1, keepdims=True)
    both = jnp.maximum(top, prior)
    lse2 = both + jnp.log2(summed * jnp.exp2(top - both) + jnp.exp2(prior - both))
    row = jnp.transpose(lse2)[0:1, :]
    for i in range(8):
        packed[4, i : i + 1, :] = row[:, i * 128 : (i + 1) * 128]

    def send_lse(t, to):
        return pltpu.make_async_remote_copy(
            src_ref=packed.at[4], dst_ref=packed.at[t], send_sem=s_lse.at[t], recv_sem=r_lse.at[t],
            device_id=device(to), device_id_type=MESH,
        )

    lse_sends = [send_lse(M1, near(b, 1)), send_lse(P1, near(b, -1)), send_lse(M9, near(b, 9)), send_lse(P9, near(b, -9))]
    for s in lse_sends:
        s.start()
    lcol[...] = lse2
    lnb[4, 0:1, :] = row
    lse_ref[...] = row * LN2

    def weights(t, at):
        parts = []
        mine = lcol[at, :]
        for i in range(8):
            lanes = slice(i * 128, (i + 1) * 128)
            tile = scores[t, at, lanes]
            parts.append(jnp.exp2(tile - mine) + jnp.exp2(tile - lnb[t, 0:1, lanes]))
        return parts

    prow = (partner_ref[...] % ROWS).astype(jnp.float32)
    pcol[...] = column(prow)

    def own_part(r, carry):
        at = pl.ds(pl.multiple_of(r * 512, 512), 512)
        parts = weights(4, at)
        mine = pcol[at, :]
        row = (lax.broadcasted_iota(jnp.int32, (512, 128), 0) + r * 512).astype(jnp.float32)
        lane = lax.broadcasted_iota(jnp.int32, (512, 128), 1).astype(jnp.float32)
        for i in range(8):
            lanes = slice(i * 128, (i + 1) * 128)
            hot = jnp.where(mine == lane + i * 128.0, 1.0, 0.0) + jnp.where(prow[:, lanes] == row, 1.0, 0.0)
            parts[i] = (parts[i] - hot).astype(jnp.bfloat16)
        out[at, :] = jnp.dot(jnp.concatenate(parts, axis=1), own[...], preferred_element_type=jnp.float32)
        return carry

    lax.fori_loop(0, 2, own_part, 0)

    def sent(k, carry):
        odd = by_z(k)
        @pl.when(k + AHEAD >= CHUNKS)
        def _():
            send_up(k).wait_send()
            send_dn(k).wait_send()

        send_loc(k).wait_send()

        @pl.when(far_moves(k))
        def _():
            send_far(k).wait_send()

        @pl.when(rel_dbl)
        def _():
            send_r1(k).wait_send()
            send_r9(k).wait_send()

        @pl.when(rel_sgl & ~odd)
        def _():
            send_r1(k).wait_send()

        @pl.when(z_src & aside(k))
        def _():
            send_side(k).wait_send()

        @pl.when(z_moves(k))
        def _():
            send_z(k).wait_send()

        return carry

    lax.fori_loop(0, CHUNKS, sent, 0)

    order = (P1, M1, P9, M9)
    for t in order:
        lse_sends[t].wait_recv()
        for i in range(8):
            lnb[t, 0:1, i * 128 : (i + 1) * 128] = packed[t, i : i + 1, :]

        def term(r, carry):
            at = pl.ds(pl.multiple_of(r * 512, 512), 512)
            w = jnp.concatenate([p.astype(jnp.bfloat16) for p in weights(t, at)], axis=1)
            part = jnp.dot(w, buf[t], preferred_element_type=jnp.float32)
            if t in (M1, M9):
                part = part.astype(jnp.bfloat16).astype(jnp.float32)
            acc = out[at, :] + part
            out[at, :] = SCALE * acc if t == order[-1] else acc
            return carry

        lax.fori_loop(0, ROWS // 512, term, 0, unroll=True)

    for s in lse_sends:
        s.wait_send()


def per_device(embeddings, partner, prior_lse):
    dma = pltpu.SemaphoreType.DMA
    f32 = jnp.float32
    gradient, lse = pl.pallas_call(
        kernel,
        out_shape=(pltpu.VMEM((ROWS, D), f32), jax.ShapeDtypeStruct((1, ROWS), f32)),
        in_specs=[
            pl.BlockSpec(memory_space=pltpu.HBM),
            pl.BlockSpec(memory_space=pltpu.VMEM),
            pl.BlockSpec(memory_space=pltpu.VMEM),
        ],
        out_specs=(pl.BlockSpec(memory_space=pltpu.VMEM), pl.BlockSpec(memory_space=pltpu.VMEM)),
        scratch_shapes=[
            pltpu.VMEM((ROWS, D), jnp.bfloat16),
            pltpu.VMEM((6, ROWS, D), jnp.bfloat16),
            pltpu.VMEM((5, ROWS, ROWS), f32),
            pltpu.VMEM((ROWS, 128), f32),
            pltpu.VMEM((ROWS, 128), f32),
            pltpu.VMEM((ROWS, 128), f32),
            pltpu.VMEM((ROWS, 128), f32),
            pltpu.VMEM((5, 8, ROWS), f32),
            pltpu.VMEM((5, 8, 128), f32),
            dma, dma((CHUNKS,)), dma((CHUNKS,)), dma((CHUNKS,)), dma((CHUNKS,)), dma((CHUNKS,)),
            dma((CHUNKS,)), dma((CHUNKS,)), dma((4,)), dma((4,)), dma((6, CHUNKS)),
        ],
        compiler_params=pltpu.CompilerParams(collective_id=0, has_side_effects=True, vmem_limit_bytes=56 << 20),
        cost_estimate=pl.CostEstimate(flops=20 * ROWS * ROWS * D, bytes_accessed=8 << 20, transcendentals=20 << 20),
    )(embeddings, partner.reshape(1, ROWS), prior_lse.reshape(1, ROWS))
    return gradient, lse.reshape(ROWS)


def solution(mesh):
    placed = (P(("dp", "sub"), None), P(("dp", "sub")), P(("dp", "sub")))
    return jax.shard_map(
        per_device,
        mesh=mesh,
        in_specs=placed,
        out_specs=(P(("dp", "sub"), None), P(("dp", "sub"))),
        check_vma=False,
    )
```
